512 devices in a mesh: grp: 32 (over z_hi, y, core), vocab: 16 (over z_lo, x).
Axes of the slice: x: 4, y: 4, z: 16 (z_hi: 4, z_lo: 4; z = z_hi * 4 + z_lo), core: 2. Of those that a mesh axis runs over, the one named last changes fastest.
Arguments:
- t_act: bfloat16 [192, 25600], P(None, 'vocab'), may hold values from -6 to 6
- t_down: bfloat16 [25600, 5120], P('vocab', 'grp'), may hold values from -0.0390625 to 0.0390625
- t_resid: bfloat16 [192, 5120], P('vocab', 'grp'), may hold values from -6 to 6
- t_gain: float32 [5120], P('grp'), may hold values from 0.25 to 1.75
- s_hidden: bfloat16 [192, 4096], P('vocab', 'grp'), may hold values from -6 to 6
- t_head: bfloat16 [98304, 5120], P(('grp', 'vocab')), may hold values from -30 to 30
- s_head: bfloat16 [98304, 4096], P(('grp', 'vocab')), may hold values from -30 to 30
- domain_ids: int32 [192], replicated, may hold values from 0 to 7
- domain_counts: int32 [8], replicated, may hold values from 12 to 47
Outputs:
- grad_hidden: float32 [192, 4096], P('vocab', 'grp')
- domain_loss: float32 [8], replicated
The draws below stay inside these ranges and needn't reach their ends.
All inputs are finite; a program needn't handle non-finite values.
Results may differ from the reference program's by a relative error of at most 0.0067.
Values may be sent and summed in bfloat16 or wider, within the bound.
A program may use at most 64 MiB of HBM per device.

```python
import math
import jax
import jax.numpy as jnp
from jax import lax

DT = 5120
DS = 4096
FFT = 25600
TOK = 192
NDOM = 8
VOCAB = 98304


def draw_t_head(key, part):
    key = jax.random.fold_in(key, 11)
    first = jax.random.fold_in(key, 0)
    table = jax.random.normal(first, (VOCAB, DT), jnp.float32) * (3.0 / math.sqrt(DT))
    return jnp.clip(table, -30.0, 30.0).astype(jnp.bfloat16)


def draw_s_head(key, part):
    key = jax.random.fold_in(key, 23)
    first = jax.random.fold_in(key, 0)
    table = jax.random.normal(first, (VOCAB, DS), jnp.float32) * (3.0 / math.sqrt(DS))
    return jnp.clip(table, -30.0, 30.0).astype(jnp.bfloat16)


def plant(values, key, least, top_value):
    place = [jax.random.randint(jax.random.fold_in(key, axis), (), 0, length) for axis, length in enumerate(values.shape)]
    longest = values.shape.index(max(values.shape))
    beside = place[:longest] + [(place[longest] + 1) % values.shape[longest]] + place[longest + 1:]
    return values.at[tuple(place)].set(least).at[tuple(beside)].set(top_value)


def levels(rng, extent, shards, smallest, top_value):
    def one(position, shards_of):
        heights = jax.random.uniform(jax.random.fold_in(jax.random.fold_in(rng, 6), position), (shards_of,), jnp.float32, smallest / len(shards), top_value / len(shards))
        return jnp.repeat(jnp.exp(heights), extent[position] // shards_of).reshape((-1,) + (1,) * (len(extent) - position - 1))

    gain = one(*shards[0])
    for cut in shards[1:]:
        gain = gain * one(*cut)
    return gain


def gaussian(stream_key, dims, width, limit, cuts=(), held_as=jnp.bfloat16):
    values = jax.random.normal(stream_key, dims, jnp.float32) * width
    if len(cuts) > 0:
        values = levels(stream_key, dims, cuts, -0.22, 0.18) * values
    return jnp.clip(values, min=-limit, max=limit).astype(held_as)


def setup_inputs(seed: int = 0) -> dict:
    arg_keys = jax.random.split(jax.random.key(seed), 10)
    t_act = gaussian(arg_keys[0], (TOK, FFT), 1.0, 6.0, ((1, 16),))
    t_down = gaussian(arg_keys[1], (FFT, DT), FFT ** -0.5, 0.0390625, ((0, 16), (1, 32)))
    t_resid = gaussian(arg_keys[2], (TOK, DT), 1.0, 6.0, ((0, 16), (1, 32)))
    t_gain = jnp.clip(1.0 + 0.15 * jax.random.normal(arg_keys[3], (DT,), jnp.float32), 0.25, 1.75)
    s_hidden = gaussian(arg_keys[4], (TOK, DS), 1.0, 6.0, ((0, 16), (1, 32)))
    t_head = draw_t_head(jax.random.fold_in(arg_keys[9], 71), 0)
    s_head = draw_s_head(jax.random.fold_in(arg_keys[9], 71), 0)
    domain_ids = plant(jax.random.randint(arg_keys[7], (TOK,), 0, NDOM), jax.random.fold_in(arg_keys[7], 1), 0, NDOM - 1).astype(jnp.int32)
    domain_counts = plant(jax.random.randint(arg_keys[8], (NDOM,), TOK // (2 * NDOM), 2 * TOK // NDOM), jax.random.fold_in(arg_keys[8], 1), TOK // (2 * NDOM), (2 * TOK // NDOM) - 1).astype(jnp.int32)
    return dict(t_act=t_act, t_down=t_down, t_resid=t_resid, t_gain=t_gain, s_hidden=s_hidden, t_head=t_head, s_head=s_head, domain_ids=domain_ids, domain_counts=domain_counts)


def logits_of(hidden, head):
    return lax.dot_general(hidden, head, (((1,), (1,)), ((), ())), preferred_element_type=jnp.float32)

def reference(t_act, t_down, t_resid, t_gain, s_hidden, t_head, s_head, domain_ids, domain_counts):
    pre = t_resid.astype(jnp.float32) + jnp.dot(t_act, t_down, preferred_element_type=jnp.float32)
    meansq = lax.optimization_barrier(jnp.mean(pre * pre, axis=1, keepdims=True))
    t_norm = (pre * lax.rsqrt(meansq + 1e-06) * t_gain[None, :]).astype(jnp.bfloat16)
    zt = logits_of(t_norm, t_head)
    zs = logits_of(s_hidden, s_head)
    top_t = lax.optimization_barrier(jnp.max(zt, axis=1, keepdims=True))
    top_s = lax.optimization_barrier(jnp.max(zs, axis=1, keepdims=True))
    exp_t = jnp.exp(zt - top_t)
    exp_s = jnp.exp(zs - top_s)
    sum_t = lax.optimization_barrier(jnp.sum(exp_t, axis=1))
    sum_s = lax.optimization_barrier(jnp.sum(exp_s, axis=1))
    cross = lax.optimization_barrier(jnp.sum(exp_t * (zt - zs), axis=1))
    kl = cross / sum_t - top_t[:, 0] - jnp.log(sum_t) + top_s[:, 0] + jnp.log(sum_s)
    onehot = (domain_ids[:, None] == jnp.arange(NDOM, dtype=jnp.int32)[None, :]).astype(jnp.float32)
    counted = lax.optimization_barrier(jnp.sum(onehot * domain_counts.astype(jnp.float32)[None, :], axis=1))
    weight = TOK / NDOM / counted
    domain_loss = lax.optimization_barrier(jnp.sum(onehot * (weight * kl)[:, None], axis=0))
    dlogit = (weight[:, None] * (exp_s / sum_s[:, None] - exp_t / sum_t[:, None])).astype(jnp.bfloat16)
    grad_hidden = jnp.dot(dlogit, s_head, preferred_element_type=jnp.float32)
    return (grad_hidden, domain_loss)
```

```python
import jax
import jax.numpy as jnp
from jax import lax
from jax.experimental import pallas as pl
from jax.experimental.pallas import tpu as pltpu
from jax.sharding import PartitionSpec as P

DT = 5120
DS = 4096
TOK = 192
NDOM = 8
F32 = jnp.float32
BF16 = jnp.bfloat16
MESH = pl.DeviceIdType.MESH
NSEM = 160
NT = (((1,), (1,)), ((), ()))
TN = (((0,), (0,)), ((), ()))


def iota(shape, axis):
    return lax.broadcasted_iota(jnp.int32, shape, axis)


class Links:
    def __init__(self, send, recv):
        self.send, self.recv, self.used, self.all = send, recv, 0, []

    def start(self, src, dst, device):
        k = self.used
        self.used += 1
        copy = pltpu.make_async_remote_copy(
            src_ref=src, dst_ref=dst, send_sem=self.send.at[k], recv_sem=self.recv.at[k],
            device_id=device, device_id_type=MESH,
        )
        copy.start()
        self.all.append(copy)
        return copy

    def finish(self):
        for copy in self.all:
            copy.wait_send()


def arrived(copies):
    for copy in copies:
        copy.wait_recv()


def merge(parts):
    mt, ms = parts[0][0:1], parts[0][3:4]
    for p in parts[1:]:
        mt, ms = jnp.maximum(mt, p[0:1]), jnp.maximum(ms, p[3:4])
    st = at = ss = None
    for p in parts:
        ft, fs = jnp.exp(p[0:1] - mt), jnp.exp(p[3:4] - ms)
        a, b, d = p[1:2] * ft, p[2:3] * ft, p[4:5] * fs
        st, at, ss = (a, b, d) if st is None else (st + a, at + b, ss + d)
    return mt, st, at, ms, ss


def put_stats(ref, stats):
    for row, value in enumerate(stats):
        ref[row : row + 1, :] = value


def body(
    act_hbm, down_hbm, resid_hbm, gain_hbm, hid_hbm, thead_hbm, shead_hbm, ids_hbm, counts,
    grad_out, loss_out,
    act, down, resid, gain, hid, thead, shead, ids,
    pmain, prem, ppack, psend, precv, pk, rem, rs, gs, u1, u2,
    hp, tz, tg, sg, q1, q2, q3,
    gsend, grecv, gown, gx, rxa, ryb, rya, rxb, sa, sb, fin, fsend, rzl, zsend, rzh,
    load_sem, send_sem, recv_sem,
):
    g, v = lax.axis_index("grp"), lax.axis_index("vocab")
    zh, y, c = g // 8, (g // 2) % 4, g % 2
    zl, x = v // 4, v % 4
    q = g % 8

    def at_x(d):
        return (g, zl * 4 + (x + d) % 4)

    def at_y(d):
        return (zh * 8 + ((y + d) % 4) * 2 + c, v)

    def at_zl(d):
        return (g, ((zl + d) % 4) * 4 + x)

    def at_zh(d):
        return (((zh + d) % 4) * 8 + q, v)

    def at_v(d):
        return (g, (v + d) % 16)

    def at_q(d):
        return (zh * 8 + (q + d) % 8, v)

    sibling = (zh * 8 + y * 2 + (1 - c), v)

    loads = {}
    for k, (name, src, dst) in enumerate((
        ("hid", hid_hbm, hid), ("act", act_hbm, act), ("down", down_hbm, down), ("resid", resid_hbm, resid),
        ("gain", gain_hbm, gain), ("ids", ids_hbm, ids), ("thead", thead_hbm, thead), ("shead", shead_hbm, shead),
    )):
        loads[name] = pltpu.make_async_copy(src, dst, load_sem.at[k])
        loads[name].start()

    barrier = pltpu.get_barrier_semaphore()
    for d in range(1, 16):
        pl.semaphore_signal(barrier, inc=1, device_id=at_v(d), device_id_type=MESH)
    for d in range(1, 8):
        pl.semaphore_signal(barrier, inc=1, device_id=at_q(d), device_id_type=MESH)
    for d in range(1, 4):
        pl.semaphore_signal(barrier, inc=1, device_id=at_zh(d), device_id_type=MESH)

    links = Links(send_sem, recv_sem)

    loads["hid"].wait()
    mine = sg.at[c, y, x, zl, zh]
    mine[...] = jnp.zeros((16, 128), BF16)
    mine[0:12, :] = hid[...]

    loads["act"].wait()
    loads["down"].wait()
    part = jnp.dot(act[...], down[...], preferred_element_type=F32)
    pmain[...] = part[:, 0:128]
    prem[:, 0:32] = part[:, 128:160]
    lane48 = iota((48, 128), 1) // 32
    packed = jnp.zeros((48, 128), F32)
    for k in range(4):
        rows = prem[pl.ds(k, 48, stride=4), :]
        rows = rows if k == 0 else pltpu.roll(rows, 32 * k, 1)
        packed = jnp.where(lane48 == k, rows, packed)
    ppack[...] = packed
    for vv in range(16):
        psend[vv, 0:12, :] = pmain[12 * vv : 12 * vv + 12, :]
        psend[vv, 12:15, :] = ppack[3 * vv : 3 * vv + 3, :]
        psend[vv, 15:16, :] = jnp.zeros((1, 128), F32)

    pl.semaphore_wait(barrier, 25)

    sums = [links.start(psend.at[(v + d) % 16], precv.at[d - 1], at_v(d)) for d in range(1, 16)]
    s_zh = [links.start(mine, mine, at_zh(d)) for d in range(1, 4)]

    loads["resid"].wait()
    loads["gain"].wait()
    rs[...] = jnp.zeros((16, 256), F32)
    rs[0:12, 0:160] = resid[...].astype(F32)
    gs[...] = jnp.zeros((1, 256), F32)
    gs[:, 0:160] = gain[...]
    rem[...] = jnp.zeros((16, 128), F32)

    arrived(s_zh)
    run = sg.at[c, y, x, zl]
    s_zl = [links.start(run, run, at_zl(d)) for d in range(1, 4)]

    arrived(sums)
    total = psend[v]
    for d in range(15):
        total = total + precv[d]
    pk[...] = total
    for k in range(4):
        rows = total[12:15, :] if k == 0 else pltpu.roll(total, 128 - 32 * k, 1)[12:15, :]
        for j in range(3):
            rem[4 * j + k : 4 * j + k + 1, 0:32] = rows[j : j + 1, 0:32]
    pre_a = jnp.where(iota((16, 128), 0) < 12, total, 0.0) + rs[:, 0:128]
    pre_b = rem[...] + rs[:, 128:256]
    diagonal = iota((16, 128), 0) == iota((16, 128), 1)
    column = jnp.sum(pre_a * pre_a + pre_b * pre_b, axis=1, keepdims=True)
    u1[q] = jnp.sum(jnp.where(diagonal, column, 0.0), axis=0, keepdims=True)
    squares = [links.start(u1.at[q], u1.at[q], at_q(d)) for d in range(1, 8)]

    def spread(buf, lo, hi):
        one = buf.at[c, y, x, pl.ds(0, 2)]
        two = buf.at[c, y, x, pl.ds(2, 2)]
        a = [links.start(one, one, at_x(d)) for d in range(1, 4)]
        b = [links.start(two, two, at_y(d)) for d in range(1, 4)]
        return a, b

    def spread_on(buf):
        one = buf.at[c, y, :, pl.ds(0, 2)]
        two = buf.at[c, :, x, pl.ds(2, 2)]
        a = [links.start(one, one, at_y(d)) for d in range(1, 4)]
        b = [links.start(two, two, at_x(d)) for d in range(1, 4)]
        return a, b, [links.start(one, one, sibling), links.start(two, two, sibling)]

    def hand_over(buf, a, b, core):
        for d in range(1, 4):
            a[d - 1].wait_recv()
            one = buf.at[c, (y + 4 - d) % 4, :, pl.ds(0, 2)]
            core.append(links.start(one, one, sibling))
            b[d - 1].wait_recv()
            two = buf.at[c, :, (x + 4 - d) % 4, pl.ds(2, 2)]
            core.append(links.start(two, two, sibling))

    arrived(s_zl)
    s_a, s_b = spread(sg, 0, 2)

    arrived(squares)
    line = u1[0]
    for k in range(1, 8):
        line = line + u1[k]
    u2[zh] = line
    squares = [links.start(u2.at[zh], u2.at[zh], at_zh(d)) for d in range(1, 4)]

    arrived(squares)
    line = (u2[0] + u2[1]) + (u2[2] + u2[3])
    column = jnp.sum(jnp.where(diagonal, line, 0.0), axis=1, keepdims=True)
    scale = lax.rsqrt(column / DT + 1e-06)
    norm_a = pre_a * scale * gs[:, 0:128]
    norm_b = pre_b * scale * gs[:, 128:256]
    moved = norm_b
    for h in range(1, 4):
        moved = jnp.where(zh == h, pltpu.roll(norm_b, 32 * h, 1), moved)
    tz[zh, 0] = norm_a.astype(BF16)
    tz[zh, 1] = moved.astype(BF16)
    t_zh = [links.start(tz.at[zh], tz.at[zh], at_zh(d)) for d in range(1, 4)]

    arrived(s_a)
    arrived(s_b)
    s_a, s_b, s_core = spread_on(sg)

    arrived(t_zh)
    for h in range(4):
        tg[c, y, x, zl, h] = tz[h, 0]
    tg[c, y, x, zl, 4] = ((tz[0, 1].astype(F32) + tz[1, 1].astype(F32)) + (tz[2, 1].astype(F32) + tz[3, 1].astype(F32))).astype(BF16)
    run = tg.at[c, y, x, zl]
    t_zl = [links.start(run, run, at_zl(d)) for d in range(1, 4)]

    hand_over(sg, s_a, s_b, s_core)

    arrived(t_zl)
    t_a, t_b = spread(tg, 0, 2)

    loads["thead"].wait()
    lane = iota((192, 128), 1)
    for qq in range(8):
        last = jnp.zeros((192, 128), F32)
        off = 32 * (qq % 4)
        for h in range(4):
            first = ((h * 8 + qq) * 160) // 128
            right = thead[:, (first + 1) * 128 : (first + 2) * 128].astype(F32)
            if off == 0:
                hp[qq, h] = thead[:, first * 128 : (first + 1) * 128]
            else:
                left = thead[:, first * 128 : (first + 1) * 128].astype(F32)
                joined = jnp.where(lane < off, right, left)
                hp[qq, h] = pltpu.roll(joined, 128 - off, 1).astype(BF16)
            shift = (32 * h - off) % 128
            moved = right if shift == 0 else pltpu.roll(right, shift, 1)
            last = jnp.where(lane // 32 == h, moved, last)
        hp[qq, 4] = last.astype(BF16)

    arrived(t_a)
    arrived(t_b)
    t_a, t_b, t_core = spread_on(tg)
    hand_over(tg, t_a, t_b, t_core)

    def rows_of(buf, cc, yy, j):
        return buf[cc, yy, :, :, j].reshape(256, 128)

    def student(cc, acc):
        for yy in range(4):
            left = jnp.concatenate(
                [shead[:, pl.ds(pl.multiple_of((h * 8 + yy * 2 + cc) * 128, 128), 128)] for h in range(4)], axis=1)
            right = jnp.concatenate([rows_of(sg, cc, yy, h) for h in range(4)], axis=1)
            one = lax.dot_general(left, right, NT, preferred_element_type=F32)
            acc = one if acc is None else acc + one
        return acc

    def teacher(cc, acc):
        for yy in range(4):
            left = jnp.concatenate([hp[yy * 2 + cc, j] for j in range(5)], axis=1)
            right = jnp.concatenate([rows_of(tg, cc, yy, j) for j in range(5)], axis=1)
            one = lax.dot_general(left, right, NT, preferred_element_type=F32)
            acc = one if acc is None else acc + one
        return acc

    loads["shead"].wait()
    zs = student(c, None)
    arrived(s_core)
    zs = student(1 - c, zs)
    zt = teacher(c, None)
    arrived(t_core)
    zt = teacher(1 - c, zt)

    mt = jnp.max(zt, axis=0, keepdims=True)
    ms = jnp.max(zs, axis=0, keepdims=True)
    et = jnp.exp(zt - mt)
    stats = (
        mt,
        jnp.sum(et, axis=0, keepdims=True),
        jnp.sum(et * (zt - zs), axis=0, keepdims=True),
        ms,
        jnp.sum(jnp.exp(zs - ms), axis=0, keepdims=True),
    )
    blank = jnp.zeros((8, 256), F32)
    for buf, slot, count, peer in ((q1, v, 16, at_v), (q2, q, 8, at_q), (q3, zh, 4, at_zh)):
        own = buf.at[slot]
        own[...] = blank
        put_stats(own, stats)
        arrived([links.start(own, own, peer(d)) for d in range(1, count)])
        stats = merge([buf[k] for k in range(count)])
    mt, st, at, ms, ss = stats

    loads["ids"].wait()
    spot = iota((192, 256), 1)
    token = ((spot // 16) % 4 * 4 + spot // 64) * 12 + spot % 16
    chosen = jnp.where((token == iota((192, 256), 0)) & (spot % 16 < 12), 1.0, 0.0).astype(BF16)
    domain = jnp.dot(
        jnp.broadcast_to(ids[...], (8, 192)).astype(F32).astype(BF16), chosen, preferred_element_type=F32)[0:1]
    counted = jnp.zeros((1, 256), F32)
    for k in range(NDOM):
        counted = jnp.where(domain == float(k), counts[k].astype(F32), counted)
    weight = TOK / NDOM / counted

    dl = (jnp.exp(zs - ms) * (weight / ss) - jnp.exp(zt - mt) * (weight / st)).astype(BF16)

    def blocks(cc, yy):
        right = jnp.concatenate(
            [shead[:, pl.ds(pl.multiple_of((h * 8 + yy * 2 + cc) * 128, 128), 128)] for h in range(4)], axis=1)
        return lax.dot_general(dl, right, TN, preferred_element_type=F32)

    over = []
    for yy in range(4):
        piece = blocks(1 - c, yy)
        for h in range(4):
            gsend[yy, :, :, h] = piece[:, h * 128 : h * 128 + 128].astype(BF16).reshape(4, 4, 16, 128)
        over.append(links.start(gsend.at[yy], grecv.at[yy], sibling))
    for yy in range(4):
        piece = blocks(c, yy)
        for h in range(4):
            gown[yy, :, :, h] = piece[:, h * 128 : h * 128 + 128].reshape(4, 4, 16, 128)

    kl = at / st - mt - jnp.log(st) + ms + jnp.log(ss)
    real = iota((1, 256), 1) % 16 < 12
    loss = jnp.zeros((1, NDOM), F32)
    for k in range(NDOM):
        one = jnp.sum(jnp.where(real & (domain == float(k)), weight * kl, 0.0), axis=1, keepdims=True)
        loss = jnp.where(iota((1, NDOM), 1) == k, one, loss)
    loss_out[...] = loss

    for yy in range(4):
        over[yy].wait_recv()
        both = gown[yy] + grecv[yy].astype(F32)
        gown[yy] = both
        gx[yy] = both.astype(BF16)
    r_a = [links.start(gx.at[:, (x + d) % 4, pl.ds(0, 2)], rxa.at[d - 1], at_x(d)) for d in range(1, 4)]
    r_b = [links.start(gx.at[(y + d) % 4, :, pl.ds(2, 2)], ryb.at[d - 1], at_y(d)) for d in range(1, 4)]

    arrived(r_a)
    acc = gown[:, x, 0:2]
    for d in range(3):
        acc = acc + rxa[d].astype(F32)
    gown[:, x, 0:2] = acc
    sa[...] = acc.astype(BF16)
    r_a = [links.start(sa.at[(y + d) % 4], rya.at[d - 1], at_y(d)) for d in range(1, 4)]
    arrived(r_b)
    acc = gown[y, :, 2:4]
    for d in range(3):
        acc = acc + ryb[d].astype(F32)
    gown[y, :, 2:4] = acc
    sb[...] = acc.astype(BF16)
    r_b = [links.start(sb.at[(x + d) % 4], rxb.at[d - 1], at_x(d)) for d in range(1, 4)]

    arrived(r_a)
    acc = gown[y, x, 0:2]
    for d in range(3):
        acc = acc + rya[d].astype(F32)
    fin[0:2] = acc
    fsend[0:2] = acc.astype(BF16)
    arrived(r_b)
    acc = gown[y, x, 2:4]
    for d in range(3):
        acc = acc + rxb[d].astype(F32)
    fin[2:4] = acc
    fsend[2:4] = acc.astype(BF16)
    arrived([links.start(fsend.at[(zl + d) % 4], rzl.at[d - 1], at_zl(d)) for d in range(1, 4)])
    acc = fin[zl]
    for d in range(3):
        acc = acc + rzl[d].astype(F32)
    fin[0] = acc
    zsend[...] = acc.astype(BF16)
    arrived([links.start(zsend.at[(zh + d) % 4], rzh.at[d - 1], at_zh(d)) for d in range(1, 4)])
    acc = fin[0, zh]
    for d in range(3):
        acc = acc + rzh[d].astype(F32)
    grad_out[...] = acc[0:12, :]
    links.finish()


def per_device(t_act, t_down, t_resid, t_gain, s_hidden, t_head, s_head, domain_ids, domain_counts):
    anywhere = pl.BlockSpec(memory_space=pl.ANY)
    held = pl.BlockSpec(memory_space=pltpu.VMEM)

    def vmem(shape, dtype=F32):
        return pltpu.VMEM(shape, dtype)

    grad, loss = pl.pallas_call(
        body,
        out_shape=(jax.ShapeDtypeStruct((12, 128), F32), jax.ShapeDtypeStruct((1, NDOM), F32)),
        in_specs=[anywhere] * 8 + [pl.BlockSpec(memory_space=pltpu.SMEM)],
        out_specs=(held, held),
        scratch_shapes=[
            vmem((192, 1600), BF16), vmem((1600, 160), BF16), vmem((12, 160), BF16), vmem((1, 160)),
            vmem((12, 128), BF16), vmem((192, DT), BF16), vmem((192, DS), BF16), vmem((1, TOK), jnp.int32),
            vmem((192, 128)), vmem((192, 128)), vmem((48, 128)),
            vmem((16, 16, 128)), vmem((15, 16, 128)), vmem((16, 128)), vmem((16, 128)),
            vmem((16, 256)), vmem((1, 256)), vmem((8, 1, 128)), vmem((4, 1, 128)),
            vmem((8, 5, 192, 128), BF16), vmem((4, 2, 16, 128), BF16),
            vmem((2, 4, 4, 4, 5, 16, 128), BF16), vmem((2, 4, 4, 4, 4, 16, 128), BF16),
            vmem((16, 8, 256)), vmem((8, 8, 256)), vmem((4, 8, 256)),
            vmem((4, 4, 4, 4, 16, 128), BF16), vmem((4, 4, 4, 4, 16, 128), BF16),
            vmem((4, 4, 4, 4, 16, 128)), vmem((4, 4, 4, 4, 16, 128), BF16),
            vmem((3, 4, 2, 4, 16, 128), BF16), vmem((3, 4, 2, 4, 16, 128), BF16),
            vmem((3, 2, 4, 16, 128), BF16), vmem((3, 2, 4, 16, 128), BF16),
            vmem((4, 2, 4, 16, 128), BF16), vmem((4, 2, 4, 16, 128), BF16),
            vmem((4, 4, 16, 128)), vmem((4, 4, 16, 128), BF16), vmem((3, 4, 16, 128), BF16),
            vmem((4, 16, 128), BF16), vmem((3, 16, 128), BF16),
            pltpu.SemaphoreType.DMA((8,)), pltpu.SemaphoreType.DMA((NSEM,)), pltpu.SemaphoreType.DMA((NSEM,)),
        ],
        compiler_params=pltpu.CompilerParams(
            collective_id=0, has_side_effects=True, vmem_limit_bytes=44 * 1024 * 1024),
    )(
        t_act, t_down, t_resid, t_gain.reshape(1, -1), s_hidden, t_head, s_head, domain_ids.reshape(1, -1),
        domain_counts,
    )
    return grad, loss.reshape(NDOM)


def solution(mesh):
    return jax.shard_map(
        per_device,
        mesh=mesh,
        in_specs=(
            P(None, "vocab"),
            P("vocab", "grp"),
            P("vocab", "grp"),
            P("grp"),
            P("vocab", "grp"),
            P(("grp", "vocab"), None),
            P(("grp", "vocab"), None),
            P(),
            P(),
        ),
        out_specs=(P("vocab", "grp"), P()),
        check_vma=False,
    )
```

```python
import jax
import jax.numpy as jnp
from jax import lax
from jax.experimental import pallas as pl
from jax.experimental.pallas import tpu as pltpu
from jax.sharding import PartitionSpec as P

DT = 5120
DS = 4096
TOK = 192
NDOM = 8
F32 = jnp.float32
BF16 = jnp.bfloat16
MESH = pl.DeviceIdType.MESH
NSEM = 160
NT = (((1,), (1,)), ((), ()))


def iota(shape, axis):
    return lax.broadcasted_iota(jnp.int32, shape, axis)


class Links:
    def __init__(self, send, recv):
        self.send, self.recv, self.used, self.all = send, recv, 0, []

    def start(self, src, dst, device):
        k = self.used
        self.used += 1
        copy = pltpu.make_async_remote_copy(
            src_ref=src, dst_ref=dst, send_sem=self.send.at[k], recv_sem=self.recv.at[k],
            device_id=device, device_id_type=MESH,
        )
        copy.start()
        self.all.append(copy)
        return copy

    def finish(self):
        for copy in self.all:
            copy.wait_send()


def arrived(copies):
    for copy in copies:
        copy.wait_recv()


def merge(buf, count):
    mt, ms = buf[0, 0], buf[0, 3]
    for k in range(1, count):
        mt, ms = jnp.maximum(mt, buf[k, 0]), jnp.maximum(ms, buf[k, 3])
    st = at = ss = jnp.zeros((1, 256), F32)
    for k in range(count):
        ft, fs = jnp.exp(buf[k, 0] - mt), jnp.exp(buf[k, 3] - ms)
        st, at, ss = st + buf[k, 1] * ft, at + buf[k, 2] * ft, ss + buf[k, 4] * fs
    return mt, st, at, ms, ss


def body(
    act_hbm, down_hbm, resid_hbm, gain_hbm, hid_hbm, thead_hbm, shead_hbm, ids_hbm, counts_hbm,
    grad_out, loss_out,
    act, down, resid, gain, hid, thead, shead, ids, counts,
    pmain, prem, ppack, psend, precv, rem, rs, gs, u1, u2,
    hp, tz, tg, sg, q1, q2, q3,
    gsend, grecv, gown, gx, rxa, ryb, rya, rxb, sa, sb, fin, fsend, rzl, zsend, rzh,
    load_sem, send_sem, recv_sem,
):
    g, v = lax.axis_index("grp"), lax.axis_index("vocab")
    zh, y, c = g // 8, (g // 2) % 4, g % 2
    zl, x = v // 4, v % 4
    q = g % 8

    def at_x(d):
        return (g, zl * 4 + (x + d) % 4)

    def at_y(d):
        return (zh * 8 + ((y + d) % 4) * 2 + c, v)

    def at_zl(d):
        return (g, ((zl + d) % 4) * 4 + x)

    def at_zh(d):
        return (((zh + d) % 4) * 8 + q, v)

    def at_v(d):
        return (g, (v + d) % 16)

    def at_q(d):
        return (zh * 8 + (q + d) % 8, v)

    sibling = (zh * 8 + y * 2 + (1 - c), v)

    loads = {}
    for k, (name, src, dst) in enumerate((
        ("hid", hid_hbm, hid), ("act", act_hbm, act), ("down", down_hbm, down), ("resid", resid_hbm, resid),
        ("gain", gain_hbm, gain), ("ids", ids_hbm, ids), ("counts", counts_hbm, counts), ("thead", thead_hbm, thead),
        ("shead", shead_hbm, shead),
    )):
        loads[name] = pltpu.make_async_copy(src, dst, load_sem.at[k])
        loads[name].start()

    barrier = pltpu.get_barrier_semaphore()
    for d in range(1, 16):
        pl.semaphore_signal(barrier, inc=1, device_id=at_v(d), device_id_type=MESH)
    for d in range(1, 8):
        pl.semaphore_signal(barrier, inc=1, device_id=at_q(d), device_id_type=MESH)
    for d in range(1, 4):
        pl.semaphore_signal(barrier, inc=1, device_id=at_zh(d), device_id_type=MESH)

    links = Links(send_sem, recv_sem)

    loads["hid"].wait()
    mine = sg.at[c, y, x, zl, zh]
    mine[...] = jnp.zeros((16, 128), BF16)
    mine[0:12, :] = hid[...]

    pl.semaphore_wait(barrier, 25)
    s_zh = [links.start(mine, mine, at_zh(d)) for d in range(1, 4)]

    loads["act"].wait()
    loads["down"].wait()
    part = lax.dot_general(act[...], down[...], NT, preferred_element_type=F32)
    pmain[...] = part[:, 0:128]
    prem[:, 0:32] = part[:, 128:160]
    lane48 = iota((48, 128), 1) // 32
    packed = jnp.zeros((48, 128), F32)
    for k in range(4):
        rows = prem[pl.ds(k, 48, stride=4), :]
        rows = rows if k == 0 else pltpu.roll(rows, 32 * k, 1)
        packed = jnp.where(lane48 == k, rows, packed)
    ppack[...] = packed
    for vv in range(16):
        psend[vv, 0:12, :] = pmain[12 * vv : 12 * vv + 12, :]
        psend[vv, 12:15, :] = ppack[3 * vv : 3 * vv + 3, :]
        psend[vv, 15:16, :] = jnp.zeros((1, 128), F32)
    sums = [links.start(psend.at[(v + d) % 16], precv.at[d - 1], at_v(d)) for d in range(1, 16)]

    loads["resid"].wait()
    loads["gain"].wait()
    rs[...] = jnp.zeros((16, 256), F32)
    rs[0:12, 0:160] = resid[...].astype(F32)
    gs[...] = jnp.zeros((1, 256), F32)
    gs[:, 0:160] = gain[...]
    rem[...] = jnp.zeros((16, 128), F32)

    arrived(s_zh)
    run = sg.at[c, y, x, zl]
    s_zl = [links.start(run, run, at_zl(d)) for d in range(1, 4)]

    loads["thead"].wait()
    lane = iota((192, 128), 1)

    def reorder(qq):
        last = jnp.zeros((192, 128), F32)
        off = 32 * (qq % 4)
        for h in range(4):
            first = ((h * 8 + qq) * 160) // 128
            right = thead[:, (first + 1) * 128 : (first + 2) * 128].astype(F32)
            if off == 0:
                hp[qq, h] = thead[:, first * 128 : (first + 1) * 128]
            else:
                left = thead[:, first * 128 : (first + 1) * 128].astype(F32)
                joined = jnp.where(lane < off, right, left)
                hp[qq, h] = pltpu.roll(joined, 128 - off, 1).astype(BF16)
            shift = (32 * h - off) % 128
            moved = right if shift == 0 else pltpu.roll(right, shift, 1)
            last = jnp.where(lane // 32 == h, moved, last)
        hp[qq, 4] = last.astype(BF16)

    reorder(0)
    reorder(1)

    arrived(sums)
    total = psend[v]
    for d in range(15):
        total = total + precv[d]
    for k in range(4):
        rows = total[12:15, :] if k == 0 else pltpu.roll(total, 128 - 32 * k, 1)[12:15, :]
        for j in range(3):
            rem[4 * j + k : 4 * j + k + 1, 0:32] = rows[j : j + 1, 0:32]
    pre_a = jnp.where(iota((16, 128), 0) < 12, total, 0.0) + rs[:, 0:128]
    pre_b = rem[...] + rs[:, 128:256]
    diagonal = iota((16, 128), 0) == iota((16, 128), 1)
    column = jnp.sum(pre_a * pre_a + pre_b * pre_b, axis=1, keepdims=True)
    u1[q] = jnp.sum(jnp.where(diagonal, column, 0.0), axis=0, keepdims=True)
    squares = [links.start(u1.at[q], u1.at[q], at_q(d)) for d in range(1, 8)]

    gained = pre_b * gs[:, 128:256]
    moved = gained
    for h in range(1, 4):
        moved = jnp.where(zh == h, pltpu.roll(gained, 32 * h, 1), moved)
    tz[zh, 0] = pre_a * gs[:, 0:128]
    tz[zh, 1] = moved
    t_zh = [links.start(tz.at[zh], tz.at[zh], at_zh(d)) for d in range(1, 4)]

    def spread(buf):
        one = buf.at[c, y, x, pl.ds(0, 2)]
        two = buf.at[c, y, x, pl.ds(2, 2)]
        a = [links.start(one, one, at_x(d)) for d in range(1, 4)]
        b = [links.start(two, two, at_y(d)) for d in range(1, 4)]
        return a, b

    def spread_on(buf, a, b):
        one = buf.at[c, y, :, pl.ds(0, 2)]
        two = buf.at[c, :, x, pl.ds(2, 2)]
        arrived(a)
        a = [links.start(one, one, at_y(d)) for d in range(1, 4)]
        arrived(b)
        b = [links.start(two, two, at_x(d)) for d in range(1, 4)]
        return a, b, [links.start(one, one, sibling), links.start(two, two, sibling)]

    def hand_over(buf, a, b, core):
        for d in (1, 3, 2):
            a[d - 1].wait_recv()
            one = buf.at[c, (y + 4 - d) % 4, :, pl.ds(0, 2)]
            core.append(links.start(one, one, sibling))
            b[d - 1].wait_recv()
            two = buf.at[c, :, (x + 4 - d) % 4, pl.ds(2, 2)]
            core.append(links.start(two, two, sibling))

    arrived(s_zl)
    s_a, s_b = spread(sg)
    reorder(2)
    reorder(3)

    arrived(squares)
    line = u1[0]
    for k in range(1, 8):
        line = line + u1[k]
    u2[zh] = line
    squares = [links.start(u2.at[zh], u2.at[zh], at_zh(d)) for d in range(1, 4)]
    s_a, s_b, s_core = spread_on(sg, s_a, s_b)
    reorder(4)
    reorder(5)

    arrived(squares)
    line = (u2[0] + u2[1]) + (u2[2] + u2[3])
    column = jnp.sum(jnp.where(diagonal, line, 0.0), axis=1, keepdims=True)
    scale = lax.rsqrt(column / DT + 1e-06)
    arrived(t_zh)
    for h in range(4):
        tg[c, y, x, zl, h] = (tz[h, 0] * scale).astype(BF16)
    tg[c, y, x, zl, 4] = (((tz[0, 1] + tz[1, 1]) + (tz[2, 1] + tz[3, 1])) * scale).astype(BF16)
    run = tg.at[c, y, x, zl]
    t_zl = [links.start(run, run, at_zl(d)) for d in range(1, 4)]
    reorder(6)
    reorder(7)

    loads["ids"].wait()
    loads["counts"].wait()
    line = iota((1, 256), 1)
    token = ((line // 16) % 4 * 4 + line // 64) * 12 + line % 16
    real = line % 16 < 12
    chosen = jnp.where(iota((192, 256), 0) == jnp.where(real, token, -1), 1.0, 0.0).astype(BF16)
    domain = jnp.dot(
        jnp.broadcast_to(ids[...], (8, 192)).astype(F32).astype(BF16), chosen, preferred_element_type=F32)[0:1]
    counted = jnp.zeros((1, 256), F32)
    for k in range(NDOM):
        counted = jnp.where(domain == float(k), counts[:, k : k + 1].astype(F32), counted)
    weight = TOK / NDOM / counted

    arrived(t_zl)
    t_a, t_b = spread(tg)
    hand_over(sg, s_a, s_b, s_core)

    def rows_of(buf, cc, yy, j):
        return buf[cc, yy, :, :, j].reshape(256, 128)

    def columns(cc, yy):
        return jnp.concatenate(
            [shead[:, pl.ds(pl.multiple_of((h * 8 + yy * 2 + cc) * 128, 128), 128)] for h in range(4)], axis=1)

    def student(cc, acc):
        for yy in range(4):
            right = jnp.concatenate([rows_of(sg, cc, yy, h) for h in range(4)], axis=1)
            one = lax.dot_general(columns(cc, yy), right, NT, preferred_element_type=F32)
            acc = one if acc is None else acc + one
        return acc

    def teacher(cc, acc):
        for yy in range(4):
            left = jnp.concatenate([hp[yy * 2 + cc, j] for j in range(5)], axis=1)
            right = jnp.concatenate([rows_of(tg, cc, yy, j) for j in range(5)], axis=1)
            one = lax.dot_general(left, right, NT, preferred_element_type=F32)
            acc = one if acc is None else acc + one
        return acc

    t_a, t_b, t_core = spread_on(tg, t_a, t_b)
    loads["shead"].wait()
    zs = student(c, None)
    arrived(s_core)
    zs = student(1 - c, zs)
    ms = jnp.max(zs, axis=0, keepdims=True)
    ss = jnp.sum(jnp.exp(zs - ms), axis=0, keepdims=True)
    hand_over(tg, t_a, t_b, t_core)
    zt = teacher(c, None)
    arrived(t_core)
    zt = teacher(1 - c, zt)

    mt = jnp.max(zt, axis=0, keepdims=True)
    et = jnp.exp(zt - mt)
    stats = (mt, jnp.sum(et, axis=0, keepdims=True), jnp.sum(et * (zt - zs), axis=0, keepdims=True), ms, ss)
    for buf, slot, count, peer in ((q1, v, 16, at_v), (q2, q, 8, at_q), (q3, zh, 4, at_zh)):
        own = buf.at[slot]
        for k in range(5):
            own[k] = stats[k]
        arrived([links.start(own, own, peer(d)) for d in range(1, count)])
        stats = merge(buf, count)
    mt, st, at, ms, ss = stats

    dl = jnp.exp(zs - ms) * (weight / ss) - jnp.exp(zt - mt) * (weight / st)
    dl = jnp.transpose(dl).astype(BF16)

    def blocks(cc, yy):
        return jnp.dot(dl, columns(cc, yy), preferred_element_type=F32)

    over = []
    for d in (1, 2, 3, 0):
        yy = (y + d) % 4
        piece = blocks(1 - c, yy)
        for h in range(4):
            gsend[yy, :, :, h] = piece[:, h * 128 : h * 128 + 128].astype(BF16).reshape(4, 4, 16, 128)
        over.append(links.start(gsend.at[yy], grecv.at[yy], sibling))
    r_b = []
    for k, d in enumerate((1, 2, 3, 0)):
        yy = (y + d) % 4
        piece = blocks(c, yy)
        over[k].wait_recv()
        for h in range(4):
            both = piece[:, h * 128 : h * 128 + 128].reshape(4, 4, 16, 128) + grecv[yy, :, :, h].astype(F32)
            gown[yy, :, :, h] = both
            gx[yy, :, :, h] = both.astype(BF16)
        if d > 0:
            r_b.append(links.start(gx.at[yy, :, pl.ds(2, 2)], ryb.at[d - 1], at_y(d)))
    r_a = [links.start(gx.at[:, (x + d) % 4, pl.ds(0, 2)], rxa.at[d - 1], at_x(d)) for d in range(1, 4)]

    arrived(r_b)
    acc = gown[y, :, 2:4]
    for d in range(3):
        acc = acc + ryb[d].astype(F32)
    gown[y, :, 2:4] = acc
    sb[...] = acc.astype(BF16)
    r_b = [links.start(sb.at[(x + d) % 4], rxb.at[d - 1], at_x(d)) for d in range(1, 4)]
    arrived(r_a)
    acc = gown[:, x, 0:2]
    for d in range(3):
        acc = acc + rxa[d].astype(F32)
    gown[:, x, 0:2] = acc
    sa[...] = acc.astype(BF16)
    r_a = [links.start(sa.at[(y + d) % 4], rya.at[d - 1], at_y(d)) for d in range(1, 4)]

    kl = at / st - mt - jnp.log(st) + ms + jnp.log(ss)
    loss = jnp.zeros((1, NDOM), F32)
    for k in range(NDOM):
        one = jnp.sum(jnp.where(real & (domain == float(k)), weight * kl, 0.0), axis=1, keepdims=True)
        loss = jnp.where(iota((1, NDOM), 1) == k, one, loss)
    loss_out[...] = loss

    arrived(r_b)
    acc = gown[y, x, 2:4]
    for d in range(3):
        acc = acc + rxb[d].astype(F32)
    fin[2:4] = acc
    fsend[2:4] = acc.astype(BF16)
    arrived(r_a)
    acc = gown[y, x, 0:2]
    for d in range(3):
        acc = acc + rya[d].astype(F32)
    fin[0:2] = acc
    fsend[0:2] = acc.astype(BF16)
    arrived([links.start(fsend.at[(zl + d) % 4], rzl.at[d - 1], at_zl(d)) for d in range(1, 4)])
    acc = fin[zl]
    for d in range(3):
        acc = acc + rzl[d].astype(F32)
    fin[0] = acc
    zsend[...] = acc.astype(BF16)
    arrived([links.start(zsend.at[(zh + d) % 4], rzh.at[d - 1], at_zh(d)) for d in range(1, 4)])
    acc = fin[0, zh]
    for d in range(3):
        acc = acc + rzh[d].astype(F32)
    grad_out[...] = acc[0:12, :]
    links.finish()


def per_device(t_act, t_down, t_resid, t_gain, s_hidden, t_head, s_head, domain_ids, domain_counts):
    anywhere = pl.BlockSpec(memory_space=pltpu.HBM)
    held = pl.BlockSpec(memory_space=pltpu.VMEM)

    def vmem(shape, dtype=F32):
        return pltpu.VMEM(shape, dtype)

    grad, loss = pl.pallas_call(
        body,
        out_shape=(jax.ShapeDtypeStruct((12, 128), F32), jax.ShapeDtypeStruct((1, NDOM), F32)),
        in_specs=[anywhere] * 9,
        out_specs=(held, held),
        scratch_shapes=[
            vmem((192, 1600), BF16), vmem((160, 1600), BF16), vmem((12, 160), BF16), vmem((1, 160)),
            vmem((12, 128), BF16), vmem((192, DT), BF16), vmem((192, DS), BF16), vmem((1, TOK), jnp.int32), vmem((1, NDOM), jnp.int32),
            vmem((192, 128)), vmem((192, 128)), vmem((48, 128)),
            vmem((16, 16, 128)), vmem((15, 16, 128)), vmem((16, 128)),
            vmem((16, 256)), vmem((1, 256)), vmem((8, 1, 128)), vmem((4, 1, 128)),
            vmem((8, 5, 192, 128), BF16), vmem((4, 2, 16, 128)),
            vmem((2, 4, 4, 4, 5, 16, 128), BF16), vmem((2, 4, 4, 4, 4, 16, 128), BF16),
            vmem((16, 5, 1, 256)), vmem((8, 5, 1, 256)), vmem((4, 5, 1, 256)),
            vmem((4, 4, 4, 4, 16, 128), BF16), vmem((4, 4, 4, 4, 16, 128), BF16),
            vmem((4, 4, 4, 4, 16, 128)), vmem((4, 4, 4, 4, 16, 128), BF16),
            vmem((3, 4, 2, 4, 16, 128), BF16), vmem((3, 4, 2, 4, 16, 128), BF16),
            vmem((3, 2, 4, 16, 128), BF16), vmem((3, 2, 4, 16, 128), BF16),
            vmem((4, 2, 4, 16, 128), BF16), vmem((4, 2, 4, 16, 128), BF16),
            vmem((4, 4, 16, 128)), vmem((4, 4, 16, 128), BF16), vmem((3, 4, 16, 128), BF16),
            vmem((4, 16, 128), BF16), vmem((3, 16, 128), BF16),
            pltpu.SemaphoreType.DMA((9,)), pltpu.SemaphoreType.DMA((NSEM,)), pltpu.SemaphoreType.DMA((NSEM,)),
        ],
        compiler_params=pltpu.CompilerParams(
            collective_id=0, has_side_effects=True, vmem_limit_bytes=62 * 1024 * 1024),
    )(
        t_act, t_down.T, t_resid, t_gain.reshape(1, -1), s_hidden, t_head, s_head, domain_ids.reshape(1, -1),
        domain_counts.reshape(1, -1),
    )
    return grad, loss.reshape(NDOM)


def solution(mesh):
    return jax.shard_map(
        per_device,
        mesh=mesh,
        in_specs=(
            P(None, "vocab"),
            P("vocab", "grp"),
            P("vocab", "grp"),
            P("grp"),
            P("vocab", "grp"),
            P(("grp", "vocab"), None),
            P(("grp", "vocab"), None),
            P(),
            P(),
        ),
        out_specs=(P("vocab", "grp"), P()),
        check_vma=False,
    )
```

```python
import jax
import jax.numpy as jnp
from jax import lax
from jax.experimental import pallas as pl
from jax.experimental.pallas import tpu as pltpu
from jax.sharding import PartitionSpec as P

DT = 5120
DS = 4096
TOK = 192
NDOM = 8
F32 = jnp.float32
BF16 = jnp.bfloat16
MESH = pl.DeviceIdType.MESH
NSEM = 192
NT = (((1,), (1,)), ((), ()))


def iota(shape, axis):
    return lax.broadcasted_iota(jnp.int32, shape, axis)


class Links:
    def __init__(self, send, recv):
        self.send, self.recv, self.used, self.all = send, recv, 0, []

    def start(self, src, dst, device):
        k = self.used
        self.used += 1
        copy = pltpu.make_async_remote_copy(
            src_ref=src, dst_ref=dst, send_sem=self.send.at[k], recv_sem=self.recv.at[k],
            device_id=device, device_id_type=MESH,
        )
        copy.start()
        self.all.append(copy)
        return copy

    def finish(self):
        for copy in self.all:
            copy.wait_send()
        self.all = []


def arrived(copies):
    for copy in copies:
        copy.wait_recv()


def merge(buf, count):
    mt, ms = buf[0, 0], buf[0, 3]
    for k in range(1, count):
        mt, ms = jnp.maximum(mt, buf[k, 0]), jnp.maximum(ms, buf[k, 3])
    st = at = ss = jnp.zeros((1, TOK), F32)
    for k in range(count):
        ft, fs = jnp.exp(buf[k, 0] - mt), jnp.exp(buf[k, 3] - ms)
        st, at, ss = st + buf[k, 1] * ft, at + buf[k, 2] * ft, ss + buf[k, 4] * fs
    return mt, st, at, ms, ss


def body(
    act_hbm, down_hbm, resid_hbm, gain_hbm, hid_hbm, thead_hbm, shead_hbm, ids_hbm, counts_hbm,
    grad_out, loss_out,
    act, down, resid, gain, hid, thead, shead, ids, counts,
    pmain, prem, ppack, psend, precv, rem, rs, gs, u1,
    hp, tz, tl, tg, sl, sg, rows48, q1, q2,
    gsend, grecv, gown, gx, rxa, ryb, rya, rxb, sa, sb, fin, zown, zsend, rz,
    load_sem, send_sem, recv_sem,
):
    g, v = lax.axis_index("grp"), lax.axis_index("vocab")
    zh, y, c = g // 8, (g // 2) % 4, g % 2
    zl, x = v // 4, v % 4
    q = g % 8

    def at_x(d):
        return (g, zl * 4 + (x + d) % 4)

    def at_y(d):
        return (zh * 8 + ((y + d) % 4) * 2 + c, v)

    def at_zl(d):
        return (g, ((zl + d) % 4) * 4 + x)

    def at_zh(d):
        return (((zh + d) % 4) * 8 + q, v)

    def at_v(d):
        return (g, (v + d) % 16)

    def at_g(d):
        return ((g + d) % 32, v)

    def at_z(a, b):
        return (((zh + a) % 4) * 8 + q, ((zl + b) % 4) * 4 + x)

    sibling = (zh * 8 + y * 2 + (1 - c), v)

    loads = {}
    for k, (name, src, dst) in enumerate((
        ("hid", hid_hbm, hid), ("act", act_hbm, act), ("down", down_hbm, down), ("resid", resid_hbm, resid),
        ("gain", gain_hbm, gain), ("ids", ids_hbm, ids), ("counts", counts_hbm, counts), ("thead", thead_hbm, thead),
        ("shead", shead_hbm, shead),
    )):
        loads[name] = pltpu.make_async_copy(src, dst, load_sem.at[k])
        loads[name].start()

    barrier = pltpu.get_barrier_semaphore()
    for d in range(1, 16):
        pl.semaphore_signal(barrier, inc=1, device_id=at_v(d), device_id_type=MESH)
    for d in range(1, 32):
        pl.semaphore_signal(barrier, inc=1, device_id=at_g(d), device_id_type=MESH)
    for a in range(1, 4):
        for b in range(1, 4):
            pl.semaphore_signal(barrier, inc=1, device_id=at_z(a, b), device_id_type=MESH)

    links = Links(send_sem, recv_sem)

    loads["hid"].wait()
    mine = sl.at[zl, zh]
    mine[...] = jnp.zeros((16, 128), BF16)
    mine[0:12, :] = hid[...]

    pl.semaphore_wait(barrier, 55)
    s_zh = [links.start(mine, mine, at_zh(d)) for d in range(1, 4)]

    loads["act"].wait()
    loads["down"].wait()
    part = lax.dot_general(act[...], down[...], NT, preferred_element_type=F32)
    pmain[...] = part[:, 0:128]
    prem[:, 0:32] = part[:, 128:160]
    lane48 = iota((48, 128), 1) // 32
    packed = jnp.zeros((48, 128), F32)
    for k in range(4):
        rows = prem[pl.ds(k, 48, stride=4), :]
        rows = rows if k == 0 else pltpu.roll(rows, 32 * k, 1)
        packed = jnp.where(lane48 == k, rows, packed)
    ppack[...] = packed
    for vv in range(16):
        psend[vv, 0:12, :] = pmain[12 * vv : 12 * vv + 12, :]
        psend[vv, 12:15, :] = ppack[3 * vv : 3 * vv + 3, :]
        psend[vv, 15:16, :] = jnp.zeros((1, 128), F32)
    sums = [links.start(psend.at[(v + d) % 16], precv.at[d - 1], at_v(d)) for d in range(1, 16)]

    loads["resid"].wait()
    loads["gain"].wait()
    rs[...] = jnp.zeros((16, 256), F32)
    rs[0:12, 0:160] = resid[...].astype(F32)
    gs[...] = jnp.zeros((1, 256), F32)
    gs[:, 0:160] = gain[...]
    rem[...] = jnp.zeros((16, 128), F32)
    zsend[...] = jnp.zeros((16, 16, 128), BF16)
    zown[...] = jnp.zeros((16, 16, 128), F32)

    arrived(s_zh)
    run = sl.at[zl]
    s_zl = [links.start(run, run, at_zl(d)) for d in range(1, 4)]

    loads["thead"].wait()
    lane = iota((192, 128), 1)

    def reorder(qq):
        last = jnp.zeros((192, 128), F32)
        off = 32 * (qq % 4)
        for h in range(4):
            first = ((h * 8 + qq) * 160) // 128
            right = thead[:, (first + 1) * 128 : (first + 2) * 128].astype(F32)
            if off == 0:
                hp[qq, h] = thead[:, first * 128 : (first + 1) * 128]
            else:
                left = thead[:, first * 128 : (first + 1) * 128].astype(F32)
                joined = jnp.where(lane < off, right, left)
                hp[qq, h] = pltpu.roll(joined, 128 - off, 1).astype(BF16)
            shift = (32 * h - off) % 128
            moved = right if shift == 0 else pltpu.roll(right, shift, 1)
            last = jnp.where(lane // 32 == h, moved, last)
        hp[qq, 4] = last.astype(BF16)

    reorder(0)
    reorder(1)

    arrived(sums)
    total = psend[v]
    for d in range(15):
        total = total + precv[d]
    for k in range(4):
        rows = total[12:15, :] if k == 0 else pltpu.roll(total, 128 - 32 * k, 1)[12:15, :]
        for j in range(3):
            rem[4 * j + k : 4 * j + k + 1, 0:32] = rows[j : j + 1, 0:32]
    pre_a = jnp.where(iota((16, 128), 0) < 12, total, 0.0) + rs[:, 0:128]
    pre_b = rem[...] + rs[:, 128:256]
    diagonal = iota((16, 128), 0) == iota((16, 128), 1)
    column = jnp.sum(pre_a * pre_a + pre_b * pre_b, axis=1, keepdims=True)
    u1[g] = jnp.sum(jnp.where(diagonal, column, 0.0), axis=0, keepdims=True)
    squares = [links.start(u1.at[g], u1.at[g], at_g(d)) for d in range(1, 32)]

    gained = pre_b * gs[:, 128:256]
    moved = gained
    for h in range(1, 4):
        moved = jnp.where(zh == h, pltpu.roll(gained, 32 * h, 1), moved)
    tz[zh, 0] = pre_a * gs[:, 0:128]
    tz[zh, 1] = moved
    t_zh = [links.start(tz.at[zh], tz.at[zh], at_zh(d)) for d in range(1, 4)]

    def pack(src, dst, tiles):
        for j in range(tiles):
            for k in range(4):
                rows48[j, 12 * k : 12 * k + 12, :] = src[k, j].astype(F32)[0:12, :]
        for j in range(tiles):
            dst[c, y, x, 3 * j : 3 * j + 3] = rows48[j].astype(BF16).reshape(3, 16, 128)

    def cut(tiles):
        half = (3 * tiles + 1) // 2
        return pl.ds(0, half), pl.ds(half, 3 * tiles - half)

    def spread(buf, tiles):
        lo, hi = cut(tiles)
        one, two = buf.at[c, y, x, lo], buf.at[c, y, x, hi]
        a = [links.start(one, one, at_x(d)) for d in range(1, 4)]
        b = [links.start(two, two, at_y(d)) for d in range(1, 4)]
        return a, b

    def spread_on(buf, tiles, a, b):
        lo, hi = cut(tiles)
        one, two = buf.at[c, y, :, lo], buf.at[c, :, x, hi]
        arrived(a)
        a = [links.start(one, one, at_y(d)) for d in range(1, 4)]
        arrived(b)
        b = [links.start(two, two, at_x(d)) for d in range(1, 4)]
        return a, b, [links.start(one, one, sibling), links.start(two, two, sibling)]

    def hand_over(buf, tiles, a, b, core):
        lo, hi = cut(tiles)
        for d in (1, 3, 2):
            a[d - 1].wait_recv()
            one = buf.at[c, (y + 4 - d) % 4, :, lo]
            core.append(links.start(one, one, sibling))
            b[d - 1].wait_recv()
            two = buf.at[c, :, (x + 4 - d) % 4, hi]
            core.append(links.start(two, two, sibling))

    arrived(s_zl)
    pack(sl, sg, 4)
    s_a, s_b = spread(sg, 4)
    reorder(2)
    reorder(3)

    arrived(squares)
    line = u1[0]
    for k in range(1, 32):
        line = line + u1[k]
    column = jnp.sum(jnp.where(diagonal, line, 0.0), axis=1, keepdims=True)
    scale = lax.rsqrt(column / DT + 1e-06)
    arrived(t_zh)
    for h in range(4):
        tl[zl, h] = (tz[h, 0] * scale).astype(BF16)
    tl[zl, 4] = (((tz[0, 1] + tz[1, 1]) + (tz[2, 1] + tz[3, 1])) * scale).astype(BF16)
    run = tl.at[zl]
    t_zl = [links.start(run, run, at_zl(d)) for d in range(1, 4)]
    s_a, s_b, s_core = spread_on(sg, 4, s_a, s_b)
    reorder(4)
    reorder(5)
    reorder(6)

    loads["ids"].wait()
    loads["counts"].wait()
    line = iota((1, TOK), 1)
    at = sum((line >= 48 * k).astype(jnp.int32) for k in range(1, 4))
    line = line - 48 * at
    run = sum((line >= 12 * k).astype(jnp.int32) for k in range(1, 4))
    token = run * 48 + at * 12 + line - 12 * run
    chosen = jnp.where(iota((TOK, TOK), 0) == token, 1.0, 0.0).astype(BF16)
    domain = jnp.dot(
        jnp.broadcast_to(ids[...], (8, TOK)).astype(F32).astype(BF16), chosen, preferred_element_type=F32)[0:1]
    counted = jnp.zeros((1, TOK), F32)
    for k in range(NDOM):
        counted = jnp.where(domain == float(k), counts[:, k : k + 1].astype(F32), counted)
    weight = TOK / NDOM / counted

    arrived(t_zl)
    pack(tl, tg, 5)
    t_a, t_b = spread(tg, 5)
    reorder(7)
    hand_over(sg, 4, s_a, s_b, s_core)

    def rows_of(buf, cc, yy, j):
        return buf[cc, yy, :, 3 * j : 3 * j + 3].reshape(TOK, 128)

    def columns(cc, yy):
        return jnp.concatenate(
            [shead[:, pl.ds(pl.multiple_of((h * 8 + yy * 2 + cc) * 128, 128), 128)] for h in range(4)], axis=1)

    def student(cc, acc):
        for yy in range(4):
            right = jnp.concatenate([rows_of(sg, cc, yy, h) for h in range(4)], axis=1)
            one = lax.dot_general(columns(cc, yy), right, NT, preferred_element_type=F32)
            acc = one if acc is None else acc + one
        return acc

    def teacher(cc, acc):
        for yy in range(4):
            left = jnp.concatenate([hp[yy * 2 + cc, j] for j in range(5)], axis=1)
            right = jnp.concatenate([rows_of(tg, cc, yy, j) for j in range(5)], axis=1)
            one = lax.dot_general(left, right, NT, preferred_element_type=F32)
            acc = one if acc is None else acc + one
        return acc

    t_a, t_b, t_core = spread_on(tg, 5, t_a, t_b)
    loads["shead"].wait()
    zs = student(c, None)
    arrived(s_core)
    zs = student(1 - c, zs)
    ms = jnp.max(zs, axis=0, keepdims=True)
    ss = jnp.sum(jnp.exp(zs - ms), axis=0, keepdims=True)
    hand_over(tg, 5, t_a, t_b, t_core)
    zt = teacher(c, None)
    arrived(t_core)
    zt = teacher(1 - c, zt)

    mt = jnp.max(zt, axis=0, keepdims=True)
    et = jnp.exp(zt - mt)
    stats = (mt, jnp.sum(et, axis=0, keepdims=True), jnp.sum(et * (zt - zs), axis=0, keepdims=True), ms, ss)
    for buf, slot, count, peer in ((q1, v, 16, at_v), (q2, g, 32, at_g)):
        own = buf.at[slot]
        for k in range(5):
            own[k] = stats[k]
        arrived([links.start(own, own, peer(d)) for d in range(1, count)])
        stats = merge(buf, count)
    mt, st, at, ms, ss = stats

    dl = jnp.exp(zs - ms) * (weight / ss) - jnp.exp(zt - mt) * (weight / st)
    dl = jnp.transpose(dl).astype(BF16)

    def blocks(cc, yy):
        return jnp.dot(dl, columns(cc, yy), preferred_element_type=F32)

    over = []
    for d in (1, 2, 3, 0):
        yy = (y + d) % 4
        piece = blocks(1 - c, yy)
        for h in range(4):
            gsend[yy, :, 3 * h : 3 * h + 3] = piece[:, h * 128 : h * 128 + 128].astype(BF16).reshape(4, 3, 16, 128)
        over.append(links.start(gsend.at[yy], grecv.at[yy], sibling))
    r_b = []
    for k, d in enumerate((1, 2, 3, 0)):
        yy = (y + d) % 4
        piece = blocks(c, yy)
        over[k].wait_recv()
        for h in range(4):
            part = pl.ds(3 * h, 3)
            both = piece[:, h * 128 : h * 128 + 128].reshape(4, 3, 16, 128) + grecv[yy, :, part].astype(F32)
            gown[yy, :, part] = both
            gx[yy, :, part] = both.astype(BF16)
        if d > 0:
            r_b.append(links.start(gx.at[yy, :, pl.ds(6, 6)], ryb.at[d - 1], at_y(d)))
    r_a = [links.start(gx.at[:, (x + d) % 4, pl.ds(0, 6)], rxa.at[d - 1], at_x(d)) for d in range(1, 4)]

    arrived(r_b)
    acc = gown[y, :, 6:12]
    for d in range(3):
        acc = acc + ryb[d].astype(F32)
    gown[y, :, 6:12] = acc
    sb[...] = acc.astype(BF16)
    r_b = [links.start(sb.at[(x + d) % 4], rxb.at[d - 1], at_x(d)) for d in range(1, 4)]
    arrived(r_a)
    acc = gown[:, x, 0:6]
    for d in range(3):
        acc = acc + rxa[d].astype(F32)
    gown[:, x, 0:6] = acc
    sa[...] = acc.astype(BF16)
    r_a = [links.start(sa.at[(y + d) % 4], rya.at[d - 1], at_y(d)) for d in range(1, 4)]

    kl = at / st - mt - jnp.log(st) + ms + jnp.log(ss)
    loss = jnp.zeros((1, NDOM), F32)
    for k in range(NDOM):
        one = jnp.sum(jnp.where(domain == float(k), weight * kl, 0.0), axis=1, keepdims=True)
        loss = jnp.where(iota((1, NDOM), 1) == k, one, loss)
    loss_out[...] = loss

    arrived(r_b)
    acc = gown[y, x, 6:12]
    for d in range(3):
        acc = acc + rxb[d].astype(F32)
    fin[2:4] = acc.reshape(2, 48, 128)
    arrived(r_a)
    acc = gown[y, x, 0:6]
    for d in range(3):
        acc = acc + rya[d].astype(F32)
    fin[0:2] = acc.reshape(2, 48, 128)

    for h in range(4):
        for k in range(4):
            rows = fin[h, 12 * k : 12 * k + 12, :]
            zown[4 * h + k, 0:12, :] = rows
            zsend[4 * h + k, 0:12, :] = rows.astype(BF16)
    last = []
    for a in range(4):
        for b in range(4):
            if a + b > 0:
                block = zsend.at[((zh + a) % 4) * 4 + (zl + b) % 4]
                last.append(links.start(block, rz.at[4 * a + b - 1], at_z(a, b)))
    links.finish()
    arrived(last)
    acc = zown[zh * 4 + zl]
    for k in range(15):
        acc = acc + rz[k].astype(F32)
    grad_out[...] = acc[0:12, :]


def per_device(t_act, t_down, t_resid, t_gain, s_hidden, t_head, s_head, domain_ids, domain_counts):
    anywhere = pl.BlockSpec(memory_space=pltpu.HBM)
    held = pl.BlockSpec(memory_space=pltpu.VMEM)

    def vmem(shape, dtype=F32):
        return pltpu.VMEM(shape, dtype)

    grad, loss = pl.pallas_call(
        body,
        out_shape=(jax.ShapeDtypeStruct((12, 128), F32), jax.ShapeDtypeStruct((1, NDOM), F32)),
        in_specs=[anywhere] * 9,
        out_specs=(held, held),
        scratch_shapes=[
            vmem((192, 1600), BF16), vmem((160, 1600), BF16), vmem((12, 160), BF16), vmem((1, 160)),
            vmem((12, 128), BF16), vmem((192, DT), BF16), vmem((192, DS), BF16), vmem((1, TOK), jnp.int32), vmem((1, NDOM), jnp.int32),
            vmem((192, 128)), vmem((192, 128)), vmem((48, 128)),
            vmem((16, 16, 128)), vmem((15, 16, 128)), vmem((16, 128)),
            vmem((16, 256)), vmem((1, 256)), vmem((32, 1, 128)),
            vmem((8, 5, 192, 128), BF16), vmem((4, 2, 16, 128)), vmem((4, 5, 16, 128), BF16),
            vmem((2, 4, 4, 15, 16, 128), BF16), vmem((4, 4, 16, 128), BF16), vmem((2, 4, 4, 12, 16, 128), BF16),
            vmem((5, 48, 128)), vmem((16, 5, 1, TOK)), vmem((32, 5, 1, TOK)),
            vmem((4, 4, 12, 16, 128), BF16), vmem((4, 4, 12, 16, 128), BF16),
            vmem((4, 4, 12, 16, 128)), vmem((4, 4, 12, 16, 128), BF16),
            vmem((3, 4, 6, 16, 128), BF16), vmem((3, 4, 6, 16, 128), BF16),
            vmem((3, 6, 16, 128), BF16), vmem((3, 6, 16, 128), BF16),
            vmem((4, 6, 16, 128), BF16), vmem((4, 6, 16, 128), BF16),
            vmem((4, 48, 128)), vmem((16, 16, 128)), vmem((16, 16, 128), BF16), vmem((15, 16, 128), BF16),
            pltpu.SemaphoreType.DMA((9,)), pltpu.SemaphoreType.DMA((NSEM,)), pltpu.SemaphoreType.DMA((NSEM,)),
        ],
        compiler_params=pltpu.CompilerParams(
            collective_id=0, has_side_effects=True, vmem_limit_bytes=62 * 1024 * 1024),
    )(
        t_act, t_down.T, t_resid, t_gain.reshape(1, -1), s_hidden, t_head, s_head, domain_ids.reshape(1, -1),
        domain_counts.reshape(1, -1),
    )
    return grad, loss.reshape(NDOM)


def solution(mesh):
    return jax.shard_map(
        per_device,
        mesh=mesh,
        in_specs=(
            P(None, "vocab"),
            P("vocab", "grp"),
            P("vocab", "grp"),
            P("grp"),
            P("vocab", "grp"),
            P(("grp", "vocab"), None),
            P(("grp", "vocab"), None),
            P(),
            P(),
        ),
        out_specs=(P("vocab", "grp"), P()),
        check_vma=False,
    )
```

```python
import jax
import jax.numpy as jnp
from jax import lax
from jax.experimental import pallas as pl
from jax.experimental.pallas import tpu as pltpu
from jax.sharding import PartitionSpec as P

DT = 5120
DS = 4096
TOK = 192
NDOM = 8
F32 = jnp.float32
BF16 = jnp.bfloat16
MESH = pl.DeviceIdType.MESH
NSEM = 192
NT = (((1,), (1,)), ((), ()))


def iota(shape, axis):
    return lax.broadcasted_iota(jnp.int32, shape, axis)


class Links:
    def __init__(self, send, recv):
        self.send, self.recv, self.used, self.all = send, recv, 0, []

    def start(self, src, dst, device):
        k = self.used
        self.used += 1
        copy = pltpu.make_async_remote_copy(
            src_ref=src, dst_ref=dst, send_sem=self.send.at[k], recv_sem=self.recv.at[k],
            device_id=device, device_id_type=MESH,
        )
        copy.start()
        self.all.append(copy)
        return copy

    def finish(self):
        for copy in self.all:
            copy.wait_send()
        self.all = []


def arrived(copies):
    for copy in copies:
        copy.wait_recv()


def merge(buf, count):
    mt, ms = buf[0, 0], buf[0, 3]
    for k in range(1, count):
        mt, ms = jnp.maximum(mt, buf[k, 0]), jnp.maximum(ms, buf[k, 3])
    st = at = ss = jnp.zeros((1, TOK), F32)
    for k in range(count):
        ft, fs = jnp.exp(buf[k, 0] - mt), jnp.exp(buf[k, 3] - ms)
        st, at, ss = st + buf[k, 1] * ft, at + buf[k, 2] * ft, ss + buf[k, 4] * fs
    return mt, st, at, ms, ss


def body(
    act_hbm, down_hbm, resid_hbm, gain_hbm, hid_hbm, thead_hbm, shead_hbm, ids_hbm, counts_hbm,
    grad_out, loss_out,
    act, down, resid, gain, hid, thead, shead, ids, counts,
    pmain, prem, ppack, psend, precv, rem, rs, gs, u1, u2,
    hp, tz, tl, tg, sl, sg, rows48, q1, q2, q3,
    gsend, grecv, gown, gx, rxa, ryb, rya, rxb, sa, sb, fin, fown, fsend, rzl, zsend, rzh,
    load_sem, send_sem, recv_sem,
):
    g, v = lax.axis_index("grp"), lax.axis_index("vocab")
    zh, q = lax.div(g, 8), lax.rem(g, 8)
    y, c = lax.div(q, 2), lax.rem(q, 2)
    zl, x = lax.div(v, 4), lax.rem(v, 4)
    xs = [x] + [lax.rem(x + d, 4) for d in range(1, 4)]
    ys = [y] + [lax.rem(y + d, 4) for d in range(1, 4)]
    zls = [zl] + [lax.rem(zl + d, 4) for d in range(1, 4)]
    zhs = [zh] + [lax.rem(zh + d, 4) for d in range(1, 4)]
    vs = [v] + [lax.rem(v + d, 16) for d in range(1, 16)]
    at_x = [(g, zl * 4 + to) for to in xs]
    at_y = [(zh * 8 + to * 2 + c, v) for to in ys]
    at_zl = [(g, to * 4 + x) for to in zls]
    at_zh = [(to * 8 + q, v) for to in zhs]
    at_v = [(g, to) for to in vs]
    at_q = [(zh * 8 + lax.rem(q + d, 8), v) for d in range(8)]
    sibling = (zh * 8 + y * 2 + (1 - c), v)

    loads = {}
    for k, (name, src, dst) in enumerate((
        ("hid", hid_hbm, hid), ("act", act_hbm, act), ("down", down_hbm, down), ("resid", resid_hbm, resid),
        ("gain", gain_hbm, gain), ("ids", ids_hbm, ids), ("counts", counts_hbm, counts), ("thead", thead_hbm, thead),
        ("shead", shead_hbm, shead),
    )):
        loads[name] = pltpu.make_async_copy(src, dst, load_sem.at[k])
        loads[name].start()

    barrier = pltpu.get_barrier_semaphore()
    for d in range(1, 16):
        pl.semaphore_signal(barrier, inc=1, device_id=at_v[d], device_id_type=MESH)
    for d in range(1, 8):
        pl.semaphore_signal(barrier, inc=1, device_id=at_q[d], device_id_type=MESH)
    for d in range(1, 4):
        pl.semaphore_signal(barrier, inc=1, device_id=at_zh[d], device_id_type=MESH)

    links = Links(send_sem, recv_sem)

    loads["hid"].wait()
    mine = sl.at[zl, zh]
    mine[...] = jnp.zeros((16, 128), BF16)
    mine[0:12, :] = hid[...]

    pl.semaphore_wait(barrier, 25)
    s_zh = [links.start(mine, mine, at_zh[d]) for d in range(1, 4)]

    loads["act"].wait()
    loads["down"].wait()
    part = lax.dot_general(act[...], down[...], NT, preferred_element_type=F32)
    pmain[...] = part[:, 0:128]
    prem[:, 0:32] = part[:, 128:160]
    lane48 = iota((48, 128), 1) // 32
    packed = jnp.zeros((48, 128), F32)
    for k in range(4):
        rows = prem[pl.ds(k, 48, stride=4), :]
        rows = rows if k == 0 else pltpu.roll(rows, 32 * k, 1)
        packed = jnp.where(lane48 == k, rows, packed)
    ppack[...] = packed
    for vv in range(16):
        psend[vv, 0:12, :] = pmain[12 * vv : 12 * vv + 12, :]
        psend[vv, 12:15, :] = ppack[3 * vv : 3 * vv + 3, :]
        psend[vv, 15:16, :] = jnp.zeros((1, 128), F32)
    sums = [links.start(psend.at[vs[d]], precv.at[d - 1], at_v[d]) for d in range(1, 16)]

    loads["resid"].wait()
    loads["gain"].wait()
    rs[...] = jnp.zeros((16, 256), F32)
    rs[0:12, 0:160] = resid[...].astype(F32)
    gs[...] = jnp.zeros((1, 256), F32)
    gs[:, 0:160] = gain[...]
    rem[...] = jnp.zeros((16, 128), F32)
    fsend[...] = jnp.zeros((4, 4, 16, 128), BF16)
    fown[...] = jnp.zeros((4, 4, 16, 128), F32)

    arrived(s_zh)
    run = sl.at[zl]
    s_zl = [links.start(run, run, at_zl[d]) for d in range(1, 4)]

    loads["thead"].wait()
    lane = iota((16, 128), 1)

    def reorder(third):
        def rows16(step, carry):
            rows = pl.ds(pl.multiple_of(third * 64 + step * 16, 16), 16)
            for qq in range(8):
                last = jnp.zeros((16, 128), F32)
                off = 32 * (qq % 4)
                for h in range(4):
                    first = ((h * 8 + qq) * 160) // 128
                    right = thead[rows, (first + 1) * 128 : (first + 2) * 128].astype(F32)
                    if off == 0:
                        hp[qq, h, rows, :] = thead[rows, first * 128 : (first + 1) * 128]
                    else:
                        left = thead[rows, first * 128 : (first + 1) * 128].astype(F32)
                        joined = jnp.where(lane < off, right, left)
                        hp[qq, h, rows, :] = pltpu.roll(joined, 128 - off, 1).astype(BF16)
                    shift = (32 * h - off) % 128
                    moved = right if shift == 0 else pltpu.roll(right, shift, 1)
                    last = jnp.where(lane // 32 == h, moved, last)
                hp[qq, 4, rows, :] = last.astype(BF16)
            return carry

        lax.fori_loop(0, 4, rows16, 0)

    reorder(0)

    arrived(sums)
    total = psend[v]
    for d in range(15):
        total = total + precv[d]
    for k in range(4):
        rows = total[12:15, :] if k == 0 else pltpu.roll(total, 128 - 32 * k, 1)[12:15, :]
        for j in range(3):
            rem[4 * j + k : 4 * j + k + 1, 0:32] = rows[j : j + 1, 0:32]
    pre_a = jnp.where(iota((16, 128), 0) < 12, total, 0.0) + rs[:, 0:128]
    pre_b = rem[...] + rs[:, 128:256]
    diagonal = iota((16, 128), 0) == iota((16, 128), 1)
    column = jnp.sum(pre_a * pre_a + pre_b * pre_b, axis=1, keepdims=True)
    u1[q] = jnp.sum(jnp.where(diagonal, column, 0.0), axis=0, keepdims=True)
    squares = [links.start(u1.at[q], u1.at[q], at_q[d]) for d in range(1, 8)]

    gained = pre_b * gs[:, 128:256]
    moved = gained
    for h in range(1, 4):
        moved = jnp.where(zh == h, pltpu.roll(gained, 32 * h, 1), moved)
    tz[zh, 0] = pre_a * gs[:, 0:128]
    tz[zh, 1] = moved
    t_zh = [links.start(tz.at[zh], tz.at[zh], at_zh[d]) for d in range(1, 4)]

    def pack(src, dst, tiles):
        for j in range(tiles):
            for k in range(4):
                rows48[j, 12 * k : 12 * k + 12, :] = src[k, j].astype(F32)[0:12, :]
        for j in range(tiles):
            dst[c, y, x, 3 * j : 3 * j + 3] = rows48[j].astype(BF16).reshape(3, 16, 128)

    def cut(tiles):
        half = (3 * tiles + 1) // 2
        return pl.ds(0, half), pl.ds(half, 3 * tiles - half)

    def spread(buf, tiles):
        lo, hi = cut(tiles)
        one, two = buf.at[c, y, x, lo], buf.at[c, y, x, hi]
        a = [links.start(one, one, at_x[d]) for d in range(1, 4)]
        b = [links.start(two, two, at_y[d]) for d in range(1, 4)]
        return a, b

    def spread_on(buf, tiles, a, b):
        lo, hi = cut(tiles)
        one, two = buf.at[c, y, :, lo], buf.at[c, :, x, hi]
        arrived(a)
        a = [links.start(one, one, at_y[d]) for d in range(1, 4)]
        arrived(b)
        b = [links.start(two, two, at_x[d]) for d in range(1, 4)]
        return a, b, [links.start(one, one, sibling), links.start(two, two, sibling)]

    def hand_over(buf, tiles, a, b, core):
        lo, hi = cut(tiles)
        for d in (1, 3, 2):
            a[d - 1].wait_recv()
            one = buf.at[c, ys[4 - d], :, lo]
            core.append(links.start(one, one, sibling))
            b[d - 1].wait_recv()
            two = buf.at[c, :, xs[4 - d], hi]
            core.append(links.start(two, two, sibling))

    arrived(s_zl)
    pack(sl, sg, 4)
    s_a, s_b = spread(sg, 4)

    arrived(squares)
    line = u1[0]
    for k in range(1, 8):
        line = line + u1[k]
    u2[zh] = line
    squares = [links.start(u2.at[zh], u2.at[zh], at_zh[d]) for d in range(1, 4)]
    s_a, s_b, s_core = spread_on(sg, 4, s_a, s_b)
    reorder(1)

    arrived(squares)
    line = (u2[0] + u2[1]) + (u2[2] + u2[3])
    column = jnp.sum(jnp.where(diagonal, line, 0.0), axis=1, keepdims=True)
    scale = lax.rsqrt(column / DT + 1e-06)
    arrived(t_zh)
    for h in range(4):
        tl[zl, h] = (tz[h, 0] * scale).astype(BF16)
    tl[zl, 4] = (((tz[0, 1] + tz[1, 1]) + (tz[2, 1] + tz[3, 1])) * scale).astype(BF16)
    run = tl.at[zl]
    t_zl = [links.start(run, run, at_zl[d]) for d in range(1, 4)]
    reorder(2)

    loads["ids"].wait()
    loads["counts"].wait()
    line = iota((1, TOK), 1)
    at = sum((line >= 48 * k).astype(jnp.int32) for k in range(1, 4))
    line = line - 48 * at
    run = sum((line >= 12 * k).astype(jnp.int32) for k in range(1, 4))
    token = run * 48 + at * 12 + line - 12 * run
    chosen = jnp.where(iota((TOK, TOK), 0) == token, 1.0, 0.0).astype(BF16)
    domain = jnp.dot(
        jnp.broadcast_to(ids[...], (8, TOK)).astype(F32).astype(BF16), chosen, preferred_element_type=F32)[0:1]
    counted = jnp.zeros((1, TOK), F32)
    for k in range(NDOM):
        counted = jnp.where(domain == float(k), counts[:, k : k + 1].astype(F32), counted)
    weight = TOK / NDOM / counted

    arrived(t_zl)
    pack(tl, tg, 5)
    t_a, t_b = spread(tg, 5)
    hand_over(sg, 4, s_a, s_b, s_core)

    def rows_of(buf, cc, yy, j):
        return buf[cc, yy, :, 3 * j : 3 * j + 3].reshape(TOK, 128)

    def columns(cc, yy):
        return jnp.concatenate(
            [shead[:, pl.ds(pl.multiple_of((h * 8 + yy * 2 + cc) * 128, 128), 128)] for h in range(4)], axis=1)

    def student(cc, acc):
        for yy in range(4):
            right = jnp.concatenate([rows_of(sg, cc, yy, h) for h in range(4)], axis=1)
            one = lax.dot_general(columns(cc, yy), right, NT, preferred_element_type=F32)
            acc = one if acc is None else acc + one
        return acc

    def teacher(cc, acc):
        for yy in range(4):
            left = jnp.concatenate([hp[yy * 2 + cc, j] for j in range(5)], axis=1)
            right = jnp.concatenate([rows_of(tg, cc, yy, j) for j in range(5)], axis=1)
            one = lax.dot_general(left, right, NT, preferred_element_type=F32)
            acc = one if acc is None else acc + one
        return acc

    t_a, t_b, t_core = spread_on(tg, 5, t_a, t_b)
    loads["shead"].wait()
    zs = student(c, None)
    arrived(s_core)
    zs = student(1 - c, zs)
    ms = jnp.max(zs, axis=0, keepdims=True)
    ss = jnp.sum(jnp.exp(zs - ms), axis=0, keepdims=True)
    hand_over(tg, 5, t_a, t_b, t_core)
    zt = teacher(c, None)
    arrived(t_core)
    zt = teacher(1 - c, zt)

    mt = jnp.max(zt, axis=0, keepdims=True)
    et = jnp.exp(zt - mt)
    stats = (mt, jnp.sum(et, axis=0, keepdims=True), jnp.sum(et * (zt - zs), axis=0, keepdims=True), ms, ss)
    for buf, slot, count, peer in ((q1, v, 16, at_v), (q2, q, 8, at_q), (q3, zh, 4, at_zh)):
        own = buf.at[slot]
        for k in range(5):
            own[k] = stats[k]
        arrived([links.start(own, own, peer[d]) for d in range(1, count)])
        stats = merge(buf, count)
    mt, st, at, ms, ss = stats

    dl = jnp.exp(zs - ms) * (weight / ss) - jnp.exp(zt - mt) * (weight / st)
    dl = jnp.transpose(dl).astype(BF16)

    def blocks(cc, yy):
        return jnp.dot(dl, columns(cc, yy), preferred_element_type=F32)

    over = []
    for d in (1, 2, 3, 0):
        yy = ys[d]
        piece = blocks(1 - c, yy)
        for h in range(4):
            gsend[yy, :, 3 * h : 3 * h + 3] = piece[:, h * 128 : h * 128 + 128].astype(BF16).reshape(4, 3, 16, 128)
        over.append(links.start(gsend.at[yy], grecv.at[yy], sibling))
    r_b = []
    for k, d in enumerate((1, 2, 3, 0)):
        yy = ys[d]
        piece = blocks(c, yy)
        over[k].wait_recv()
        for h in range(4):
            part = pl.ds(3 * h, 3)
            both = piece[:, h * 128 : h * 128 + 128].reshape(4, 3, 16, 128) + grecv[yy, :, part].astype(F32)
            gown[yy, :, part] = both
            gx[yy, :, part] = both.astype(BF16)
        if d > 0:
            r_b.append(links.start(gx.at[yy, :, pl.ds(6, 6)], ryb.at[d - 1], at_y[d]))
    r_a = [links.start(gx.at[:, xs[d], pl.ds(0, 6)], rxa.at[d - 1], at_x[d]) for d in range(1, 4)]

    arrived(r_b)
    acc = gown[y, :, 6:12]
    for d in range(3):
        acc = acc + ryb[d].astype(F32)
    gown[y, :, 6:12] = acc
    sb[...] = acc.astype(BF16)
    r_b = [links.start(sb.at[xs[d]], rxb.at[d - 1], at_x[d]) for d in range(1, 4)]
    arrived(r_a)
    acc = gown[:, x, 0:6]
    for d in range(3):
        acc = acc + rxa[d].astype(F32)
    gown[:, x, 0:6] = acc
    sa[...] = acc.astype(BF16)
    r_a = [links.start(sa.at[ys[d]], rya.at[d - 1], at_y[d]) for d in range(1, 4)]

    kl = at / st - mt - jnp.log(st) + ms + jnp.log(ss)
    loss = jnp.zeros((1, NDOM), F32)
    for k in range(NDOM):
        one = jnp.sum(jnp.where(domain == float(k), weight * kl, 0.0), axis=1, keepdims=True)
        loss = jnp.where(iota((1, NDOM), 1) == k, one, loss)
    loss_out[...] = loss

    arrived(r_b)
    acc = gown[y, x, 6:12]
    for d in range(3):
        acc = acc + rxb[d].astype(F32)
    fin[2:4] = acc.reshape(2, 48, 128)
    arrived(r_a)
    acc = gown[y, x, 0:6]
    for d in range(3):
        acc = acc + rya[d].astype(F32)
    fin[0:2] = acc.reshape(2, 48, 128)

    for h in range(4):
        for k in range(4):
            rows = fin[h, 12 * k : 12 * k + 12, :]
            fown[k, h, 0:12, :] = rows
            fsend[k, h, 0:12, :] = rows.astype(BF16)
    last = [links.start(fsend.at[zls[d]], rzl.at[d - 1], at_zl[d]) for d in range(1, 4)]
    links.finish()
    arrived(last)
    acc = fown[zl]
    for d in range(3):
        acc = acc + rzl[d].astype(F32)
    fown[0] = acc
    zsend[...] = acc.astype(BF16)
    arrived([links.start(zsend.at[zhs[d]], rzh.at[d - 1], at_zh[d]) for d in range(1, 4)])
    acc = fown[0, zh]
    for d in range(3):
        acc = acc + rzh[d].astype(F32)
    grad_out[...] = acc[0:12, :]
    links.finish()


def per_device(t_act, t_down, t_resid, t_gain, s_hidden, t_head, s_head, domain_ids, domain_counts):
    anywhere = pl.BlockSpec(memory_space=pltpu.HBM)
    held = pl.BlockSpec(memory_space=pltpu.VMEM)

    def vmem(shape, dtype=F32):
        return pltpu.VMEM(shape, dtype)

    grad, loss = pl.pallas_call(
        body,
        out_shape=(jax.ShapeDtypeStruct((12, 128), F32), jax.ShapeDtypeStruct((1, NDOM), F32)),
        in_specs=[anywhere] * 9,
        out_specs=(held, held),
        scratch_shapes=[
            vmem((192, 1600), BF16), vmem((160, 1600), BF16), vmem((12, 160), BF16), vmem((1, 160)),
            vmem((12, 128), BF16), vmem((192, DT), BF16), vmem((192, DS), BF16), vmem((1, TOK), jnp.int32), vmem((1, NDOM), jnp.int32),
            vmem((192, 128)), vmem((192, 128)), vmem((48, 128)),
            vmem((16, 16, 128)), vmem((15, 16, 128)), vmem((16, 128)),
            vmem((16, 256)), vmem((1, 256)), vmem((8, 1, 128)), vmem((4, 1, 128)),
            vmem((8, 5, 192, 128), BF16), vmem((4, 2, 16, 128)), vmem((4, 5, 16, 128), BF16),
            vmem((2, 4, 4, 15, 16, 128), BF16), vmem((4, 4, 16, 128), BF16), vmem((2, 4, 4, 12, 16, 128), BF16),
            vmem((5, 48, 128)), vmem((16, 5, 1, TOK)), vmem((8, 5, 1, TOK)), vmem((4, 5, 1, TOK)),
            vmem((4, 4, 12, 16, 128), BF16), vmem((4, 4, 12, 16, 128), BF16),
            vmem((4, 4, 12, 16, 128)), vmem((4, 4, 12, 16, 128), BF16),
            vmem((3, 4, 6, 16, 128), BF16), vmem((3, 4, 6, 16, 128), BF16),
            vmem((3, 6, 16, 128), BF16), vmem((3, 6, 16, 128), BF16),
            vmem((4, 6, 16, 128), BF16), vmem((4, 6, 16, 128), BF16),
            vmem((4, 48, 128)), vmem((4, 4, 16, 128)), vmem((4, 4, 16, 128), BF16), vmem((3, 4, 16, 128), BF16),
            vmem((4, 16, 128), BF16), vmem((3, 16, 128), BF16),
            pltpu.SemaphoreType.DMA((9,)), pltpu.SemaphoreType.DMA((NSEM,)), pltpu.SemaphoreType.DMA((NSEM,)),
        ],
        compiler_params=pltpu.CompilerParams(
            collective_id=0, has_side_effects=True, vmem_limit_bytes=62 * 1024 * 1024),
    )(
        t_act, t_down.T, t_resid, t_gain.reshape(1, -1), s_hidden, t_head, s_head, domain_ids.reshape(1, -1),
        domain_counts.reshape(1, -1),
    )
    return grad, loss.reshape(NDOM)


def solution(mesh):
    return jax.shard_map(
        per_device,
        mesh=mesh,
        in_specs=(
            P(None, "vocab"),
            P("vocab", "grp"),
            P("vocab", "grp"),
            P("grp"),
            P("vocab", "grp"),
            P(("grp", "vocab"), None),
            P(("grp", "vocab"), None),
            P(),
            P(),
        ),
        out_specs=(P("vocab", "grp"), P()),
        check_vma=False,
    )
```

```python
import jax
import jax.numpy as jnp
from jax import lax
from jax.experimental import pallas as pl
from jax.experimental.pallas import tpu as pltpu
from jax.sharding import PartitionSpec as P

DT = 5120
DS = 4096
TOK = 192
NDOM = 8
F32 = jnp.float32
BF16 = jnp.bfloat16
MESH = pl.DeviceIdType.MESH
NSEM = 192
NT = (((1,), (1,)), ((), ()))


def iota(shape, axis):
    return lax.broadcasted_iota(jnp.int32, shape, axis)


class Links:
    def __init__(self, send, recv):
        self.send, self.recv, self.used, self.all = send, recv, 0, []

    def at(self, k, src, dst, device):
        return pltpu.make_async_remote_copy(
            src_ref=src, dst_ref=dst, send_sem=self.send.at[k], recv_sem=self.recv.at[k],
            device_id=device, device_id_type=MESH,
        )

    def start(self, src, dst, device):
        copy = self.at(self.used, src, dst, device)
        self.used += 1
        copy.start()
        self.all.append(copy)
        return copy

    def group(self, count, describe):
        first = self.used
        self.used += count
        copies = [self.at(first + k, *describe(k)) for k in range(count)]
        self.all += copies
        return first, copies

    def finish(self):
        for copy in self.all:
            copy.wait_send()
        self.all = []


def arrived(copies):
    for copy in copies:
        copy.wait_recv()


def merge(buf, count):
    mt, ms = buf[0, 0], buf[0, 3]
    for k in range(1, count):
        mt, ms = jnp.maximum(mt, buf[k, 0]), jnp.maximum(ms, buf[k, 3])
    st = at = ss = jnp.zeros((1, TOK), F32)
    for k in range(count):
        ft, fs = jnp.exp(buf[k, 0] - mt), jnp.exp(buf[k, 3] - ms)
        st, at, ss = st + buf[k, 1] * ft, at + buf[k, 2] * ft, ss + buf[k, 4] * fs
    return mt, st, at, ms, ss


def body(
    act_hbm, down_hbm, resid_hbm, gain_hbm, hid_hbm, thead_hbm, shead_hbm, ids_hbm, counts_hbm,
    grad_out, loss_out,
    act, down, resid, gain, hid, thead, shead, ids, counts,
    pmain, prem, ppack, psend, precv, rem, rs, gs, u1, u2,
    hp, tz, tl, tg, sl, sg, rows48, q1, q2, q3, zs_ref, zt_ref, dl_ref,
    gsend, grecv, gown, gx, rxa, ryb, rya, rxb, sa, sb, fin, fown, fsend, rzl, zsend, rzh,
    load_sem, send_sem, recv_sem,
):
    g, v = lax.axis_index("grp"), lax.axis_index("vocab")
    zh, q = lax.div(g, 8), lax.rem(g, 8)
    y, c = lax.div(q, 2), lax.rem(q, 2)
    zl, x = lax.div(v, 4), lax.rem(v, 4)
    xs = [x] + [lax.rem(x + d, 4) for d in range(1, 4)]
    ys = [y] + [lax.rem(y + d, 4) for d in range(1, 4)]
    zls = [zl] + [lax.rem(zl + d, 4) for d in range(1, 4)]
    zhs = [zh] + [lax.rem(zh + d, 4) for d in range(1, 4)]
    vs = [v] + [lax.rem(v + d, 16) for d in range(1, 16)]
    at_x = [(g, zl * 4 + to) for to in xs]
    at_y = [(zh * 8 + to * 2 + c, v) for to in ys]
    at_zl = [(g, to * 4 + x) for to in zls]
    at_zh = [(to * 8 + q, v) for to in zhs]
    at_v = [(g, to) for to in vs]
    at_q = [(zh * 8 + lax.rem(q + d, 8), v) for d in range(8)]
    sibling = (zh * 8 + y * 2 + (1 - c), v)

    loads = {}
    for k, (name, src, dst) in enumerate((
        ("act", act_hbm, act), ("down", down_hbm, down), ("hid", hid_hbm, hid), ("resid", resid_hbm, resid),
        ("gain", gain_hbm, gain), ("thead", thead_hbm, thead), ("ids", ids_hbm, ids), ("counts", counts_hbm, counts),
        ("shead", shead_hbm, shead),
    )):
        loads[name] = pltpu.make_async_copy(src, dst, load_sem.at[k])
    for name in ("act", "down", "hid"):
        loads[name].start()

    barrier = pltpu.get_barrier_semaphore()
    for d in range(1, 16):
        pl.semaphore_signal(barrier, inc=1, device_id=at_v[d], device_id_type=MESH)
    for d in range(1, 8):
        pl.semaphore_signal(barrier, inc=1, device_id=at_q[d], device_id_type=MESH)
    for d in range(1, 4):
        pl.semaphore_signal(barrier, inc=1, device_id=at_zh[d], device_id_type=MESH)

    for name in ("resid", "gain", "thead", "ids", "counts", "shead"):
        loads[name].start()

    links = Links(send_sem, recv_sem)

    loads["hid"].wait()
    mine = sl.at[zl, zh]
    mine[...] = jnp.zeros((16, 128), BF16)
    mine[0:12, :] = hid[...]

    pl.semaphore_wait(barrier, 25)
    s_zh = [links.start(mine, mine, at_zh[d]) for d in range(1, 4)]

    loads["act"].wait()
    loads["down"].wait()
    part = lax.dot_general(act[...], down[...], NT, preferred_element_type=F32)
    pmain[...] = part[:, 0:128]
    prem[:, 0:32] = part[:, 128:160]
    lane48 = iota((48, 128), 1) // 32
    packed = jnp.zeros((48, 128), F32)
    for k in range(4):
        rows = prem[pl.ds(k, 48, stride=4), :]
        rows = rows if k == 0 else pltpu.roll(rows, 32 * k, 1)
        packed = jnp.where(lane48 == k, rows, packed)
    ppack[...] = packed
    for vv in range(16):
        psend[vv, 0:12, :] = pmain[12 * vv : 12 * vv + 12, :]
        psend[vv, 12:15, :] = ppack[3 * vv : 3 * vv + 3, :]
        psend[vv, 15:16, :] = jnp.zeros((1, 128), F32)
    sums = [links.start(psend.at[vs[d]], precv.at[d - 1], at_v[d]) for d in range(1, 16)]

    loads["resid"].wait()
    loads["gain"].wait()
    rs[...] = jnp.zeros((16, 256), F32)
    rs[0:12, 0:160] = resid[...].astype(F32)
    gs[...] = jnp.zeros((1, 256), F32)
    gs[:, 0:160] = gain[...]
    rem[...] = jnp.zeros((16, 128), F32)
    zs_ref[...] = jnp.zeros((192, TOK), F32)
    zt_ref[...] = jnp.zeros((192, TOK), F32)
    fsend[...] = jnp.zeros((4, 4, 16, 128), BF16)
    fown[...] = jnp.zeros((4, 4, 16, 128), F32)

    arrived(s_zh)
    run = sl.at[zl]
    s_zl = [links.start(run, run, at_zl[d]) for d in range(1, 4)]

    loads["thead"].wait()
    lane = iota((16, 128), 1)

    def reorder(third):
        def rows16(step, carry):
            rows = pl.ds(pl.multiple_of(third * 64 + step * 16, 16), 16)
            for qq in range(8):
                last = jnp.zeros((16, 128), F32)
                off = 32 * (qq % 4)
                for h in range(4):
                    first = ((h * 8 + qq) * 160) // 128
                    right = thead[rows, (first + 1) * 128 : (first + 2) * 128].astype(F32)
                    if off == 0:
                        hp[qq, h, rows, :] = thead[rows, first * 128 : (first + 1) * 128]
                    else:
                        left = thead[rows, first * 128 : (first + 1) * 128].astype(F32)
                        joined = jnp.where(lane < off, right, left)
                        hp[qq, h, rows, :] = pltpu.roll(joined, 128 - off, 1).astype(BF16)
                    shift = (32 * h - off) % 128
                    moved = right if shift == 0 else pltpu.roll(right, shift, 1)
                    last = jnp.where(lane // 32 == h, moved, last)
                hp[qq, 4, rows, :] = last.astype(BF16)
            return carry

        lax.fori_loop(0, 4, rows16, 0)

    reorder(0)

    arrived(sums)
    total = psend[v]
    for d in range(15):
        total = total + precv[d]
    for k in range(4):
        rows = total[12:15, :] if k == 0 else pltpu.roll(total, 128 - 32 * k, 1)[12:15, :]
        for j in range(3):
            rem[4 * j + k : 4 * j + k + 1, 0:32] = rows[j : j + 1, 0:32]
    pre_a = jnp.where(iota((16, 128), 0) < 12, total, 0.0) + rs[:, 0:128]
    pre_b = rem[...] + rs[:, 128:256]
    diagonal = iota((16, 128), 0) == iota((16, 128), 1)
    column = jnp.sum(pre_a * pre_a + pre_b * pre_b, axis=1, keepdims=True)
    u1[q] = jnp.sum(jnp.where(diagonal, column, 0.0), axis=0, keepdims=True)
    squares = [links.start(u1.at[q], u1.at[q], at_q[d]) for d in range(1, 8)]

    gained = pre_b * gs[:, 128:256]
    moved = gained
    for h in range(1, 4):
        moved = jnp.where(zh == h, pltpu.roll(gained, 32 * h, 1), moved)
    tz[zh, 0] = pre_a * gs[:, 0:128]
    tz[zh, 1] = moved
    t_zh = [links.start(tz.at[zh], tz.at[zh], at_zh[d]) for d in range(1, 4)]

    def pack(src, dst, tiles):
        for j in range(tiles):
            for k in range(4):
                rows48[j, 12 * k : 12 * k + 12, :] = src[k, j].astype(F32)[0:12, :]
        for j in range(tiles):
            dst[c, y, x, 3 * j : 3 * j + 3] = rows48[j].astype(BF16).reshape(3, 16, 128)

    def cut(tiles):
        half = (3 * tiles + 1) // 2
        return pl.ds(0, half), pl.ds(half, 3 * tiles - half)

    def spread(buf, tiles):
        lo, hi = cut(tiles)
        one, two = buf.at[c, y, x, lo], buf.at[c, y, x, hi]
        a = [links.start(one, one, at_x[d]) for d in range(1, 4)]
        b = [links.start(two, two, at_y[d]) for d in range(1, 4)]
        return a, b

    def spread_on(buf, tiles, a, b):
        lo, hi = cut(tiles)
        one, two = buf.at[c, y, :, lo], buf.at[c, :, x, hi]
        arrived(a)
        a = [links.start(one, one, at_y[d]) for d in range(1, 4)]
        arrived(b)
        b = [links.start(two, two, at_x[d]) for d in range(1, 4)]
        return a, b, [links.start(one, one, sibling), links.start(two, two, sibling)]

    def hand_over(buf, tiles, a, b, core):
        lo, hi = cut(tiles)
        for d in (1, 3, 2):
            a[d - 1].wait_recv()
            one = buf.at[c, ys[4 - d], :, lo]
            core.append(links.start(one, one, sibling))
            b[d - 1].wait_recv()
            two = buf.at[c, :, xs[4 - d], hi]
            core.append(links.start(two, two, sibling))

    arrived(s_zl)
    pack(sl, sg, 4)
    s_a, s_b = spread(sg, 4)

    arrived(squares)
    line = u1[0]
    for k in range(1, 8):
        line = line + u1[k]
    u2[zh] = line
    squares = [links.start(u2.at[zh], u2.at[zh], at_zh[d]) for d in range(1, 4)]
    s_a, s_b, s_core = spread_on(sg, 4, s_a, s_b)
    reorder(1)

    arrived(squares)
    line = (u2[0] + u2[1]) + (u2[2] + u2[3])
    column = jnp.sum(jnp.where(diagonal, line, 0.0), axis=1, keepdims=True)
    scale = lax.rsqrt(column / DT + 1e-06)
    arrived(t_zh)
    for h in range(4):
        tl[zl, h] = (tz[h, 0] * scale).astype(BF16)
    tl[zl, 4] = (((tz[0, 1] + tz[1, 1]) + (tz[2, 1] + tz[3, 1])) * scale).astype(BF16)
    run = tl.at[zl]
    t_zl = [links.start(run, run, at_zl[d]) for d in range(1, 4)]
    reorder(2)

    loads["ids"].wait()
    loads["counts"].wait()
    line = iota((1, TOK), 1)
    at = sum((line >= 48 * k).astype(jnp.int32) for k in range(1, 4))
    line = line - 48 * at
    run = sum((line >= 12 * k).astype(jnp.int32) for k in range(1, 4))
    token = run * 48 + at * 12 + line - 12 * run
    chosen = jnp.where(iota((TOK, TOK), 0) == token, 1.0, 0.0).astype(BF16)
    domain = jnp.dot(
        jnp.broadcast_to(ids[...], (8, TOK)).astype(F32).astype(BF16), chosen, preferred_element_type=F32)[0:1]
    counted = jnp.zeros((1, TOK), F32)
    for k in range(NDOM):
        counted = jnp.where(domain == float(k), counts[:, k : k + 1].astype(F32), counted)
    weight = TOK / NDOM / counted

    arrived(t_zl)
    pack(tl, tg, 5)
    t_a, t_b = spread(tg, 5)
    hand_over(sg, 4, s_a, s_b, s_core)

    def rows_of(buf, cc, yy, j):
        return buf[cc, yy, :, 3 * j : 3 * j + 3].reshape(TOK, 128)

    def columns(cc, yy):
        return jnp.concatenate(
            [shead[:, pl.ds(pl.multiple_of((h * 8 + yy * 2 + cc) * 128, 128), 128)] for h in range(4)], axis=1)

    def student(cc):
        def one(yy, carry):
            right = jnp.concatenate([rows_of(sg, cc, yy, h) for h in range(4)], axis=1)
            zs_ref[...] += lax.dot_general(columns(cc, yy), right, NT, preferred_element_type=F32)
            return carry

        lax.fori_loop(0, 4, one, 0)

    def teacher(cc):
        def one(yy, carry):
            left = jnp.concatenate([hp[yy * 2 + cc, j] for j in range(5)], axis=1)
            right = jnp.concatenate([rows_of(tg, cc, yy, j) for j in range(5)], axis=1)
            zt_ref[...] += lax.dot_general(left, right, NT, preferred_element_type=F32)
            return carry

        lax.fori_loop(0, 4, one, 0)

    t_a, t_b, t_core = spread_on(tg, 5, t_a, t_b)
    loads["shead"].wait()
    student(c)
    arrived(s_core)
    student(1 - c)
    zs = zs_ref[...]
    ms = jnp.max(zs, axis=0, keepdims=True)
    ss = jnp.sum(jnp.exp(zs - ms), axis=0, keepdims=True)
    hand_over(tg, 5, t_a, t_b, t_core)
    teacher(c)
    arrived(t_core)
    teacher(1 - c)
    zs, zt = zs_ref[...], zt_ref[...]
    mt = jnp.max(zt, axis=0, keepdims=True)
    et = jnp.exp(zt - mt)
    stats = (mt, jnp.sum(et, axis=0, keepdims=True), jnp.sum(et * (zt - zs), axis=0, keepdims=True), ms, ss)
    for buf, slot, count, peer in ((q1, v, 16, at_v), (q2, q, 8, at_q), (q3, zh, 4, at_zh)):
        own = buf.at[slot]
        for k in range(5):
            own[k] = stats[k]
        arrived([links.start(own, own, peer[d]) for d in range(1, count)])
        stats = merge(buf, count)
    mt, st, at, ms, ss = stats

    zs, zt = zs_ref[...], zt_ref[...]
    dl = jnp.exp(zs - ms) * (weight / ss) - jnp.exp(zt - mt) * (weight / st)
    dl_ref[...] = jnp.transpose(dl).astype(BF16)

    def blocks(cc, yy):
        return jnp.dot(dl_ref[...], columns(cc, yy), preferred_element_type=F32)

    def row(k):
        return lax.rem(y + k + 1, 4)

    def to_other(k):
        return gsend.at[row(k)], grecv.at[row(k)], sibling

    def along_y(k):
        return gx.at[row(k), :, pl.ds(6, 6)], ryb.at[k], (zh * 8 + row(k) * 2 + c, v)

    o_first, over = links.group(4, to_other)
    b_first, r_b = links.group(3, along_y)

    def give(k, carry):
        piece = blocks(1 - c, row(k))
        for h in range(4):
            gsend[row(k), :, 3 * h : 3 * h + 3] = piece[:, h * 128 : h * 128 + 128].astype(BF16).reshape(4, 3, 16, 128)
        links.at(o_first + k, *to_other(k)).start()
        return carry

    def keep(k, carry):
        piece = blocks(c, row(k))
        links.at(o_first + k, *to_other(k)).wait_recv()
        for h in range(4):
            part = pl.ds(3 * h, 3)
            both = piece[:, h * 128 : h * 128 + 128].reshape(4, 3, 16, 128) + grecv[row(k), :, part].astype(F32)
            gown[row(k), :, part] = both
            gx[row(k), :, part] = both.astype(BF16)

        @pl.when(k < 3)
        def _():
            links.at(b_first + k, *along_y(k)).start()

        return carry

    lax.fori_loop(0, 4, give, 0)
    lax.fori_loop(0, 4, keep, 0)
    r_a = [links.start(gx.at[:, xs[d], pl.ds(0, 6)], rxa.at[d - 1], at_x[d]) for d in range(1, 4)]

    arrived(r_b)
    acc = gown[y, :, 6:12]
    for d in range(3):
        acc = acc + ryb[d].astype(F32)
    gown[y, :, 6:12] = acc
    sb[...] = acc.astype(BF16)
    r_b = [links.start(sb.at[xs[d]], rxb.at[d - 1], at_x[d]) for d in range(1, 4)]
    arrived(r_a)
    acc = gown[:, x, 0:6]
    for d in range(3):
        acc = acc + rxa[d].astype(F32)
    gown[:, x, 0:6] = acc
    sa[...] = acc.astype(BF16)
    r_a = [links.start(sa.at[ys[d]], rya.at[d - 1], at_y[d]) for d in range(1, 4)]

    kl = at / st - mt - jnp.log(st) + ms + jnp.log(ss)
    loss = jnp.zeros((1, NDOM), F32)
    for k in range(NDOM):
        one = jnp.sum(jnp.where(domain == float(k), weight * kl, 0.0), axis=1, keepdims=True)
        loss = jnp.where(iota((1, NDOM), 1) == k, one, loss)
    loss_out[...] = loss

    arrived(r_b)
    acc = gown[y, x, 6:12]
    for d in range(3):
        acc = acc + rxb[d].astype(F32)
    fin[2:4] = acc.reshape(2, 48, 128)
    arrived(r_a)
    acc = gown[y, x, 0:6]
    for d in range(3):
        acc = acc + rya[d].astype(F32)
    fin[0:2] = acc.reshape(2, 48, 128)

    for h in range(4):
        for k in range(4):
            rows = fin[h, 12 * k : 12 * k + 12, :]
            fown[k, h, 0:12, :] = rows
            fsend[k, h, 0:12, :] = rows.astype(BF16)
    last = [links.start(fsend.at[zls[d]], rzl.at[d - 1], at_zl[d]) for d in range(1, 4)]
    links.finish()
    arrived(last)
    acc = fown[zl]
    for d in range(3):
        acc = acc + rzl[d].astype(F32)
    fown[0] = acc
    zsend[...] = acc.astype(BF16)
    arrived([links.start(zsend.at[zhs[d]], rzh.at[d - 1], at_zh[d]) for d in range(1, 4)])
    acc = fown[0, zh]
    for d in range(3):
        acc = acc + rzh[d].astype(F32)
    grad_out[...] = acc[0:12, :]
    links.finish()


def per_device(t_act, t_down, t_resid, t_gain, s_hidden, t_head, s_head, domain_ids, domain_counts):
    anywhere = pl.BlockSpec(memory_space=pltpu.HBM)
    held = pl.BlockSpec(memory_space=pltpu.VMEM)

    def vmem(shape, dtype=F32):
        return pltpu.VMEM(shape, dtype)

    grad, loss = pl.pallas_call(
        body,
        out_shape=(jax.ShapeDtypeStruct((12, 128), F32), jax.ShapeDtypeStruct((1, NDOM), F32)),
        in_specs=[anywhere] * 9,
        out_specs=(held, held),
        scratch_shapes=[
            vmem((192, 1600), BF16), vmem((160, 1600), BF16), vmem((12, 160), BF16), vmem((1, 160)),
            vmem((12, 128), BF16), vmem((192, DT), BF16), vmem((192, DS), BF16), vmem((1, TOK), jnp.int32), vmem((1, NDOM), jnp.int32),
            vmem((192, 128)), vmem((192, 128)), vmem((48, 128)),
            vmem((16, 16, 128)), vmem((15, 16, 128)), vmem((16, 128)),
            vmem((16, 256)), vmem((1, 256)), vmem((8, 1, 128)), vmem((4, 1, 128)),
            vmem((8, 5, 192, 128), BF16), vmem((4, 2, 16, 128)), vmem((4, 5, 16, 128), BF16),
            vmem((2, 4, 4, 15, 16, 128), BF16), vmem((4, 4, 16, 128), BF16), vmem((2, 4, 4, 12, 16, 128), BF16),
            vmem((5, 48, 128)), vmem((16, 5, 1, TOK)), vmem((8, 5, 1, TOK)), vmem((4, 5, 1, TOK)),
            vmem((192, TOK)), vmem((192, TOK)), vmem((TOK, 192), BF16),
            vmem((4, 4, 12, 16, 128), BF16), vmem((4, 4, 12, 16, 128), BF16),
            vmem((4, 4, 12, 16, 128)), vmem((4, 4, 12, 16, 128), BF16),
            vmem((3, 4, 6, 16, 128), BF16), vmem((3, 4, 6, 16, 128), BF16),
            vmem((3, 6, 16, 128), BF16), vmem((3, 6, 16, 128), BF16),
            vmem((4, 6, 16, 128), BF16), vmem((4, 6, 16, 128), BF16),
            vmem((4, 48, 128)), vmem((4, 4, 16, 128)), vmem((4, 4, 16, 128), BF16), vmem((3, 4, 16, 128), BF16),
            vmem((4, 16, 128), BF16), vmem((3, 16, 128), BF16),
            pltpu.SemaphoreType.DMA((9,)), pltpu.SemaphoreType.DMA((NSEM,)), pltpu.SemaphoreType.DMA((NSEM,)),
        ],
        compiler_params=pltpu.CompilerParams(
            collective_id=0, has_side_effects=True, vmem_limit_bytes=62 * 1024 * 1024),
    )(
        t_act, t_down.T, t_resid, t_gain.reshape(1, -1), s_hidden, t_head, s_head, domain_ids.reshape(1, -1),
        domain_counts.reshape(1, -1),
    )
    return grad, loss.reshape(NDOM)


def solution(mesh):
    return jax.shard_map(
        per_device,
        mesh=mesh,
        in_specs=(
            P(None, "vocab"),
            P("vocab", "grp"),
            P("vocab", "grp"),
            P("grp"),
            P("vocab", "grp"),
            P(("grp", "vocab"), None),
            P(("grp", "vocab"), None),
            P(),
            P(),
        ),
        out_specs=(P("vocab", "grp"), P()),
        check_vma=False,
    )
```

```python
import jax
import jax.numpy as jnp
from jax import lax
from jax.experimental import pallas as pl
from jax.experimental.pallas import tpu as pltpu
from jax.sharding import PartitionSpec as P

DT = 5120
DS = 4096
TOK = 192
NDOM = 8
F32 = jnp.float32
BF16 = jnp.bfloat16
MESH = pl.DeviceIdType.MESH
NSEM = 192
NT = (((1,), (1,)), ((), ()))


def iota(shape, axis):
    return lax.broadcasted_iota(jnp.int32, shape, axis)


class Links:
    def __init__(self, send, recv):
        self.send, self.recv, self.used, self.all = send, recv, 0, []

    def at(self, k, src, dst, device):
        return pltpu.make_async_remote_copy(
            src_ref=src, dst_ref=dst, send_sem=self.send.at[k], recv_sem=self.recv.at[k],
            device_id=device, device_id_type=MESH,
        )

    def start(self, src, dst, device):
        copy = self.at(self.used, src, dst, device)
        self.used += 1
        copy.start()
        self.all.append(copy)
        return copy

    def group(self, count, describe):
        first = self.used
        self.used += count
        copies = [self.at(first + k, *describe(k)) for k in range(count)]
        self.all += copies
        return first, copies

    def finish(self):
        for copy in self.all:
            copy.wait_send()
        self.all = []


def arrived(copies):
    for copy in copies:
        copy.wait_recv()


def merge(buf, count):
    mt, ms = buf[0, 0], buf[0, 3]
    for k in range(1, count):
        mt, ms = jnp.maximum(mt, buf[k, 0]), jnp.maximum(ms, buf[k, 3])
    st = at = ss = jnp.zeros((1, TOK), F32)
    for k in range(count):
        ft, fs = jnp.exp(buf[k, 0] - mt), jnp.exp(buf[k, 3] - ms)
        st, at, ss = st + buf[k, 1] * ft, at + buf[k, 2] * ft, ss + buf[k, 4] * fs
    return mt, st, at, ms, ss


def body(
    act_hbm, down_hbm, resid_hbm, gain_hbm, hid_hbm, thead_hbm, shead_hbm, ids_hbm, counts_hbm,
    grad_out, loss_out,
    act, down, resid, gain, hid, thead, shead, ids, counts,
    pmain, prem, ppack, psend, precv, rem, rs, rp, gs, u1, u2,
    hp, tz, tl, tg, sl, sg, rows48, q1, q2, q3, zs_ref, zt_ref, dl_ref,
    gsend, grecv, gown, gx, rxa, ryb, rya, rxb, sa, sb, fin, fown, fsend, rzl, zsend, rzh,
    load_sem, send_sem, recv_sem,
):
    g, v = lax.axis_index("grp"), lax.axis_index("vocab")
    zh, q = lax.div(g, 8), lax.rem(g, 8)
    y, c = lax.div(q, 2), lax.rem(q, 2)
    zl, x = lax.div(v, 4), lax.rem(v, 4)
    xs = [x] + [lax.rem(x + d, 4) for d in range(1, 4)]
    ys = [y] + [lax.rem(y + d, 4) for d in range(1, 4)]
    zls = [zl] + [lax.rem(zl + d, 4) for d in range(1, 4)]
    zhs = [zh] + [lax.rem(zh + d, 4) for d in range(1, 4)]
    vs = [v] + [lax.rem(v + d, 16) for d in range(1, 16)]
    at_x = [(g, zl * 4 + to) for to in xs]
    at_y = [(zh * 8 + to * 2 + c, v) for to in ys]
    at_zl = [(g, to * 4 + x) for to in zls]
    at_zh = [(to * 8 + q, v) for to in zhs]
    at_v = [(g, to) for to in vs]
    at_q = [(zh * 8 + lax.rem(q + d, 8), v) for d in range(8)]
    sibling = (zh * 8 + y * 2 + (1 - c), v)

    loads = {}
    for k, (name, src, dst) in enumerate((
        ("act", act_hbm, act), ("down", down_hbm, down), ("hid", hid_hbm, hid), ("resid", resid_hbm, resid),
        ("gain", gain_hbm, gain), ("thead", thead_hbm, thead), ("ids", ids_hbm, ids), ("counts", counts_hbm, counts),
        ("shead", shead_hbm, shead),
    )):
        loads[name] = pltpu.make_async_copy(src, dst, load_sem.at[k])
    for name in ("act", "down", "hid"):
        loads[name].start()

    barrier = pltpu.get_barrier_semaphore()
    for d in range(1, 16):
        pl.semaphore_signal(barrier, inc=1, device_id=at_v[d], device_id_type=MESH)
    for d in range(1, 8):
        pl.semaphore_signal(barrier, inc=1, device_id=at_q[d], device_id_type=MESH)
    for d in range(1, 4):
        pl.semaphore_signal(barrier, inc=1, device_id=at_zh[d], device_id_type=MESH)

    for name in ("resid", "gain", "thead", "ids", "counts", "shead"):
        loads[name].start()

    links = Links(send_sem, recv_sem)

    loads["hid"].wait()
    mine = sl.at[zl, zh]
    mine[...] = jnp.zeros((16, 128), BF16)
    mine[0:12, :] = hid[...]

    pl.semaphore_wait(barrier, 25)
    s_zh = [links.start(mine, mine, at_zh[d]) for d in range(1, 4)]

    loads["act"].wait()
    loads["down"].wait()
    part = lax.dot_general(act[...], down[...], NT, preferred_element_type=F32)
    pmain[...] = part[:, 0:128]
    prem[:, 0:32] = part[:, 128:160]
    lane48 = iota((48, 128), 1) // 32
    packed = jnp.zeros((48, 128), F32)
    for k in range(4):
        rows = prem[pl.ds(k, 48, stride=4), :]
        rows = rows if k == 0 else pltpu.roll(rows, 32 * k, 1)
        packed = jnp.where(lane48 == k, rows, packed)
    ppack[...] = packed
    for vv in range(16):
        psend[vv, 0:12, :] = pmain[12 * vv : 12 * vv + 12, :]
        psend[vv, 12:15, :] = ppack[3 * vv : 3 * vv + 3, :]
        psend[vv, 15:16, :] = jnp.zeros((1, 128), F32)
    sums = [links.start(psend.at[vs[d]], precv.at[d - 1], at_v[d]) for d in range(1, 16)]

    loads["resid"].wait()
    loads["gain"].wait()
    group = iota((16, 128), 1) // 32
    rs[...] = jnp.zeros((16, 256), F32)
    rs[0:12, 0:160] = resid[...].astype(F32)
    gs[...] = jnp.zeros((1, 256), F32)
    gs[:, 0:160] = gain[...]
    four = gs[:, 128:256]
    four = four + pltpu.roll(four, 32, 1)
    four = four + pltpu.roll(four, 64, 1)
    gains = jnp.where(iota((16, 128), 0) < 12, gs[:, 0:128], four)
    rp[...] = rs[:, 0:128]
    for j in range(3):
        line = rs[4 * j : 4 * j + 1, 128:256]
        for k in range(1, 4):
            line = line + pltpu.roll(rs[4 * j + k : 4 * j + k + 1, 128:256], 32 * k, 1)
        rp[12 + j : 13 + j, :] = line
    rem[...] = jnp.zeros((16, 128), F32)
    zs_ref[...] = jnp.zeros((192, TOK), F32)
    zt_ref[...] = jnp.zeros((192, TOK), F32)
    fsend[...] = jnp.zeros((4, 4, 16, 128), BF16)
    fown[...] = jnp.zeros((4, 4, 16, 128), F32)

    arrived(s_zh)
    run = sl.at[zl]
    s_zl = [links.start(run, run, at_zl[d]) for d in range(1, 4)]

    loads["thead"].wait()
    lane = iota((16, 128), 1)

    def reorder(third):
        def rows16(step, carry):
            rows = pl.ds(pl.multiple_of(third * 64 + step * 16, 16), 16)
            for qq in range(8):
                last = jnp.zeros((16, 128), F32)
                off = 32 * (qq % 4)
                for h in range(4):
                    first = ((h * 8 + qq) * 160) // 128
                    right = thead[rows, (first + 1) * 128 : (first + 2) * 128].astype(F32)
                    if off == 0:
                        hp[qq, h, rows, :] = thead[rows, first * 128 : (first + 1) * 128]
                    else:
                        left = thead[rows, first * 128 : (first + 1) * 128].astype(F32)
                        joined = jnp.where(lane < off, right, left)
                        hp[qq, h, rows, :] = pltpu.roll(joined, 128 - off, 1).astype(BF16)
                    shift = (32 * h - off) % 128
                    moved = right if shift == 0 else pltpu.roll(right, shift, 1)
                    last = jnp.where(lane // 32 == h, moved, last)
                hp[qq, 4, rows, :] = last.astype(BF16)
            return carry

        lax.fori_loop(0, 4, rows16, 0)

    reorder(0)

    def pack(src, dst, tiles):
        for j in range(tiles):
            for k in range(4):
                rows48[j, 12 * k : 12 * k + 12, :] = src[k, j].astype(F32)[0:12, :]
        for j in range(tiles):
            dst[c, y, x, 3 * j : 3 * j + 3] = rows48[j].astype(BF16).reshape(3, 16, 128)

    def cut(tiles):
        half = (3 * tiles + 1) // 2
        return pl.ds(0, half), pl.ds(half, 3 * tiles - half)

    def spread(buf, tiles):
        lo, hi = cut(tiles)
        one, two = buf.at[c, y, x, lo], buf.at[c, y, x, hi]
        a = [links.start(one, one, at_x[d]) for d in range(1, 4)]
        b = [links.start(two, two, at_y[d]) for d in range(1, 4)]
        return a, b

    def spread_on(buf, tiles, a, b):
        lo, hi = cut(tiles)
        one, two = buf.at[c, y, :, lo], buf.at[c, :, x, hi]
        arrived(a)
        a = [links.start(one, one, at_y[d]) for d in range(1, 4)]
        arrived(b)
        b = [links.start(two, two, at_x[d]) for d in range(1, 4)]
        return a, b, [links.start(one, one, sibling), links.start(two, two, sibling)]

    def hand_over(buf, tiles, a, b, core):
        lo, hi = cut(tiles)
        for d in (1, 3, 2):
            a[d - 1].wait_recv()
            one = buf.at[c, ys[4 - d], :, lo]
            core.append(links.start(one, one, sibling))
            b[d - 1].wait_recv()
            two = buf.at[c, :, xs[4 - d], hi]
            core.append(links.start(two, two, sibling))

    arrived(s_zl)
    pack(sl, sg, 4)
    s_a, s_b = spread(sg, 4)

    arrived(sums)
    total = psend[v]
    for d in range(15):
        total = total + precv[d]
    pre = total + rp[...]
    square = pre * pre
    row_of, lane_of = iota((16, 128), 0), iota((16, 128), 1)
    diagonal = row_of == lane_of
    line = jnp.where(diagonal & (row_of < 12), jnp.sum(square, axis=1, keepdims=True), 0.0)
    for k in range(4):
        column = jnp.sum(jnp.where(group == k, square, 0.0), axis=1, keepdims=True)
        line = line + jnp.where((row_of >= 12) & (lane_of == 4 * row_of - 48 + k), column, 0.0)
    u1[q] = jnp.sum(line, axis=0, keepdims=True)
    squares = [links.start(u1.at[q], u1.at[q], at_q[d]) for d in range(1, 8)]

    tz[zh] = pre * gains
    t_zh = [links.start(tz.at[zh], tz.at[zh], at_zh[d]) for d in range(1, 4)]

    arrived(squares)
    line = u1[0]
    for k in range(1, 8):
        line = line + u1[k]
    u2[zh] = line
    squares = [links.start(u2.at[zh], u2.at[zh], at_zh[d]) for d in range(1, 4)]
    s_a, s_b, s_core = spread_on(sg, 4, s_a, s_b)
    reorder(1)

    arrived(t_zh)
    for k in range(4):
        side = jnp.zeros((8, 128), F32)
        for h in range(4):
            tail = tz[h, 8:16, :]
            tail = tail if h == k else pltpu.roll(tail, 32 * ((h - k) % 4), 1)
            side = jnp.where(iota((8, 128), 1) // 32 == h, tail, side)
        for j in range(3):
            rem[4 * j + k : 4 * j + k + 1, :] = side[4 + j : 5 + j, :]

    arrived(squares)
    line = (u2[0] + u2[1]) + (u2[2] + u2[3])
    column = jnp.sum(jnp.where(diagonal, line, 0.0), axis=1, keepdims=True)
    scale = lax.rsqrt(column / DT + 1e-06)
    for h in range(4):
        tl[zl, h] = (tz[h] * scale).astype(BF16)
    tl[zl, 4] = (rem[...] * scale).astype(BF16)
    run = tl.at[zl]
    t_zl = [links.start(run, run, at_zl[d]) for d in range(1, 4)]
    reorder(2)

    loads["ids"].wait()
    loads["counts"].wait()
    line = iota((1, TOK), 1)
    at = sum((line >= 48 * k).astype(jnp.int32) for k in range(1, 4))
    line = line - 48 * at
    run = sum((line >= 12 * k).astype(jnp.int32) for k in range(1, 4))
    token = run * 48 + at * 12 + line - 12 * run
    chosen = jnp.where(iota((TOK, TOK), 0) == token, 1.0, 0.0).astype(BF16)
    domain = jnp.dot(
        jnp.broadcast_to(ids[...], (8, TOK)).astype(F32).astype(BF16), chosen, preferred_element_type=F32)[0:1]
    counted = jnp.zeros((1, TOK), F32)
    for k in range(NDOM):
        counted = jnp.where(domain == float(k), counts[:, k : k + 1].astype(F32), counted)
    weight = TOK / NDOM / counted

    arrived(t_zl)
    pack(tl, tg, 5)
    t_a, t_b = spread(tg, 5)
    hand_over(sg, 4, s_a, s_b, s_core)

    def rows_of(buf, cc, yy, j):
        return buf[cc, yy, :, 3 * j : 3 * j + 3].reshape(TOK, 128)

    def columns(cc, yy):
        return jnp.concatenate(
            [shead[:, pl.ds(pl.multiple_of((h * 8 + yy * 2 + cc) * 128, 128), 128)] for h in range(4)], axis=1)

    def student(cc):
        def one(yy, carry):
            right = jnp.concatenate([rows_of(sg, cc, yy, h) for h in range(4)], axis=1)
            zs_ref[...] += lax.dot_general(columns(cc, yy), right, NT, preferred_element_type=F32)
            return carry

        lax.fori_loop(0, 4, one, 0)

    def teacher(cc):
        def two(half, carry):
            pairs = [(half * 2 + k, j) for k in range(2) for j in range(5)]
            left = jnp.concatenate([hp[yy * 2 + cc, j] for yy, j in pairs], axis=1)
            right = jnp.concatenate([rows_of(tg, cc, yy, j) for yy, j in pairs], axis=1)
            zt_ref[...] += lax.dot_general(left, right, NT, preferred_element_type=F32)
            return carry

        lax.fori_loop(0, 2, two, 0)

    t_a, t_b, t_core = spread_on(tg, 5, t_a, t_b)
    loads["shead"].wait()
    student(c)
    arrived(s_core)
    student(1 - c)
    zs = zs_ref[...]
    ms = jnp.max(zs, axis=0, keepdims=True)
    ss = jnp.sum(jnp.exp(zs - ms), axis=0, keepdims=True)
    hand_over(tg, 5, t_a, t_b, t_core)
    teacher(c)
    arrived(t_core)
    teacher(1 - c)
    zs, zt = zs_ref[...], zt_ref[...]
    mt = jnp.max(zt, axis=0, keepdims=True)
    et = jnp.exp(zt - mt)
    stats = (mt, jnp.sum(et, axis=0, keepdims=True), jnp.sum(et * (zt - zs), axis=0, keepdims=True), ms, ss)
    for buf, slot, count, peer in ((q1, v, 16, at_v), (q2, q, 8, at_q), (q3, zh, 4, at_zh)):
        own = buf.at[slot]
        for k in range(5):
            own[k] = stats[k]
        arrived([links.start(own, own, peer[d]) for d in range(1, count)])
        stats = merge(buf, count)
    mt, st, at, ms, ss = stats

    zs, zt = zs_ref[...], zt_ref[...]
    dl = jnp.exp(zs - ms) * (weight / ss) - jnp.exp(zt - mt) * (weight / st)
    dl_ref[...] = jnp.transpose(dl).astype(BF16)

    def blocks(cc, yy):
        return jnp.dot(dl_ref[...], columns(cc, yy), preferred_element_type=F32)

    def row(k):
        return lax.rem(y + k + 1, 4)

    def to_other(k):
        return gsend.at[row(k)], grecv.at[row(k)], sibling

    def along_y(k):
        return gx.at[row(k), :, pl.ds(6, 6)], ryb.at[k], (zh * 8 + row(k) * 2 + c, v)

    o_first, over = links.group(4, to_other)
    b_first, r_b = links.group(3, along_y)

    def give(k, carry):
        piece = blocks(1 - c, row(k))
        for h in range(4):
            gsend[row(k), :, 3 * h : 3 * h + 3] = piece[:, h * 128 : h * 128 + 128].astype(BF16).reshape(4, 3, 16, 128)
        links.at(o_first + k, *to_other(k)).start()
        return carry

    def keep(k, carry):
        piece = blocks(c, row(k))
        links.at(o_first + k, *to_other(k)).wait_recv()
        for h in range(4):
            part = pl.ds(3 * h, 3)
            both = piece[:, h * 128 : h * 128 + 128].reshape(4, 3, 16, 128) + grecv[row(k), :, part].astype(F32)
            gown[row(k), :, part] = both
            gx[row(k), :, part] = both.astype(BF16)

        @pl.when(k < 3)
        def _():
            links.at(b_first + k, *along_y(k)).start()

        return carry

    lax.fori_loop(0, 4, give, 0)
    lax.fori_loop(0, 4, keep, 0)
    r_a = [links.start(gx.at[:, xs[d], pl.ds(0, 6)], rxa.at[d - 1], at_x[d]) for d in range(1, 4)]

    arrived(r_b)
    acc = gown[y, :, 6:12]
    for d in range(3):
        acc = acc + ryb[d].astype(F32)
    gown[y, :, 6:12] = acc
    sb[...] = acc.astype(BF16)
    r_b = [links.start(sb.at[xs[d]], rxb.at[d - 1], at_x[d]) for d in range(1, 4)]
    arrived(r_a)
    acc = gown[:, x, 0:6]
    for d in range(3):
        acc = acc + rxa[d].astype(F32)
    gown[:, x, 0:6] = acc
    sa[...] = acc.astype(BF16)
    r_a = [links.start(sa.at[ys[d]], rya.at[d - 1], at_y[d]) for d in range(1, 4)]

    kl = at / st - mt - jnp.log(st) + ms + jnp.log(ss)
    loss = jnp.zeros((1, NDOM), F32)
    for k in range(NDOM):
        one = jnp.sum(jnp.where(domain == float(k), weight * kl, 0.0), axis=1, keepdims=True)
        loss = jnp.where(iota((1, NDOM), 1) == k, one, loss)
    loss_out[...] = loss

    arrived(r_b)
    acc = gown[y, x, 6:12]
    for d in range(3):
        acc = acc + rxb[d].astype(F32)
    fin[2:4] = acc.reshape(2, 48, 128)
    arrived(r_a)
    acc = gown[y, x, 0:6]
    for d in range(3):
        acc = acc + rya[d].astype(F32)
    fin[0:2] = acc.reshape(2, 48, 128)

    for h in range(4):
        for k in range(4):
            rows = fin[h, 12 * k : 12 * k + 12, :]
            fown[k, h, 0:12, :] = rows
            fsend[k, h, 0:12, :] = rows.astype(BF16)
    last = [links.start(fsend.at[zls[d]], rzl.at[d - 1], at_zl[d]) for d in range(1, 4)]
    links.finish()
    arrived(last)
    acc = fown[zl]
    for d in range(3):
        acc = acc + rzl[d].astype(F32)
    fown[0] = acc
    zsend[...] = acc.astype(BF16)
    arrived([links.start(zsend.at[zhs[d]], rzh.at[d - 1], at_zh[d]) for d in range(1, 4)])
    acc = fown[0, zh]
    for d in range(3):
        acc = acc + rzh[d].astype(F32)
    grad_out[...] = acc[0:12, :]
    links.finish()


def per_device(t_act, t_down, t_resid, t_gain, s_hidden, t_head, s_head, domain_ids, domain_counts):
    anywhere = pl.BlockSpec(memory_space=pltpu.HBM)
    held = pl.BlockSpec(memory_space=pltpu.VMEM)

    def vmem(shape, dtype=F32):
        return pltpu.VMEM(shape, dtype)

    grad, loss = pl.pallas_call(
        body,
        out_shape=(jax.ShapeDtypeStruct((12, 128), F32), jax.ShapeDtypeStruct((1, NDOM), F32)),
        in_specs=[anywhere] * 9,
        out_specs=(held, held),
        scratch_shapes=[
            vmem((192, 1600), BF16), vmem((160, 1600), BF16), vmem((12, 160), BF16), vmem((1, 160)),
            vmem((12, 128), BF16), vmem((192, DT), BF16), vmem((192, DS), BF16), vmem((1, TOK), jnp.int32), vmem((1, NDOM), jnp.int32),
            vmem((192, 128)), vmem((192, 128)), vmem((48, 128)),
            vmem((16, 16, 128)), vmem((15, 16, 128)), vmem((16, 128)),
            vmem((16, 256)), vmem((16, 128)), vmem((1, 256)), vmem((8, 1, 128)), vmem((4, 1, 128)),
            vmem((8, 5, 192, 128), BF16), vmem((4, 16, 128)), vmem((4, 5, 16, 128), BF16),
            vmem((2, 4, 4, 15, 16, 128), BF16), vmem((4, 4, 16, 128), BF16), vmem((2, 4, 4, 12, 16, 128), BF16),
            vmem((5, 48, 128)), vmem((16, 5, 1, TOK)), vmem((8, 5, 1, TOK)), vmem((4, 5, 1, TOK)),
            vmem((192, TOK)), vmem((192, TOK)), vmem((TOK, 192), BF16),
            vmem((4, 4, 12, 16, 128), BF16), vmem((4, 4, 12, 16, 128), BF16),
            vmem((4, 4, 12, 16, 128)), vmem((4, 4, 12, 16, 128), BF16),
            vmem((3, 4, 6, 16, 128), BF16), vmem((3, 4, 6, 16, 128), BF16),
            vmem((3, 6, 16, 128), BF16), vmem((3, 6, 16, 128), BF16),
            vmem((4, 6, 16, 128), BF16), vmem((4, 6, 16, 128), BF16),
            vmem((4, 48, 128)), vmem((4, 4, 16, 128)), vmem((4, 4, 16, 128), BF16), vmem((3, 4, 16, 128), BF16),
            vmem((4, 16, 128), BF16), vmem((3, 16, 128), BF16),
            pltpu.SemaphoreType.DMA((9,)), pltpu.SemaphoreType.DMA((NSEM,)), pltpu.SemaphoreType.DMA((NSEM,)),
        ],
        compiler_params=pltpu.CompilerParams(
            collective_id=0, has_side_effects=True, vmem_limit_bytes=62 * 1024 * 1024),
    )(
        t_act, t_down.T, t_resid, t_gain.reshape(1, -1), s_hidden, t_head, s_head, domain_ids.reshape(1, -1),
        domain_counts.reshape(1, -1),
    )
    return grad, loss.reshape(NDOM)


def solution(mesh):
    return jax.shard_map(
        per_device,
        mesh=mesh,
        in_specs=(
            P(None, "vocab"),
            P("vocab", "grp"),
            P("vocab", "grp"),
            P("grp"),
            P("vocab", "grp"),
            P(("grp", "vocab"), None),
            P(("grp", "vocab"), None),
            P(),
            P(),
        ),
        out_specs=(P("vocab", "grp"), P()),
        check_vma=False,
    )
```

```python
import jax
import jax.numpy as jnp
from jax import lax
from jax.experimental import pallas as pl
from jax.experimental.pallas import tpu as pltpu
from jax.sharding import PartitionSpec as P

DT = 5120
DS = 4096
TOK = 192
NDOM = 8
F32 = jnp.float32
BF16 = jnp.bfloat16
MESH = pl.DeviceIdType.MESH
NSEM = 192
NT = (((1,), (1,)), ((), ()))


def iota(shape, axis):
    return lax.broadcasted_iota(jnp.int32, shape, axis)


class Links:
    def __init__(self, send, recv):
        self.send, self.recv, self.used, self.all = send, recv, 0, []

    def at(self, k, src, dst, device):
        return pltpu.make_async_remote_copy(
            src_ref=src, dst_ref=dst, send_sem=self.send.at[k], recv_sem=self.recv.at[k],
            device_id=device, device_id_type=MESH,
        )

    def start(self, src, dst, device):
        copy = self.at(self.used, src, dst, device)
        self.used += 1
        copy.start()
        self.all.append(copy)
        return copy

    def group(self, count, describe):
        first = self.used
        self.used += count
        copies = [self.at(first + k, *describe(k)) for k in range(count)]
        self.all += copies
        return first, copies

    def finish(self):
        for copy in self.all:
            copy.wait_send()
        self.all = []


def arrived(copies):
    for copy in copies:
        copy.wait_recv()


def merge(buf, count):
    mt, ms = buf[0, 0], buf[0, 3]
    for k in range(1, count):
        mt, ms = jnp.maximum(mt, buf[k, 0]), jnp.maximum(ms, buf[k, 3])
    st = at = ss = jnp.zeros((1, TOK), F32)
    for k in range(count):
        ft, fs = jnp.exp(buf[k, 0] - mt), jnp.exp(buf[k, 3] - ms)
        st, at, ss = st + buf[k, 1] * ft, at + buf[k, 2] * ft, ss + buf[k, 4] * fs
    return mt, st, at, ms, ss


def body(
    act_hbm, down_hbm, resid_hbm, gain_hbm, hid_hbm, thead_hbm, shead_hbm, ids_hbm, counts_hbm,
    grad_out, loss_out,
    act, down, resid, gain, hid, thead, shead, ids, counts,
    pmain, prem, ppack, psend, precv, rem, rs, rp, gs, u1, u2,
    hp, tz, tl, tg, sl, sg, rows48, q1, q2, q3, zs_ref, zt_ref, dl_ref,
    gsend, grecv, gown, gx, rxa, ryb, rya, rxb, sa, sb, fin, fown, fsend, rzl, zsend, rzh,
    load_sem, send_sem, recv_sem,
):
    g, v = lax.axis_index("grp"), lax.axis_index("vocab")
    zh, q = lax.div(g, 8), lax.rem(g, 8)
    y, c = lax.div(q, 2), lax.rem(q, 2)
    zl, x = lax.div(v, 4), lax.rem(v, 4)
    xs = [x] + [lax.rem(x + d, 4) for d in range(1, 4)]
    ys = [y] + [lax.rem(y + d, 4) for d in range(1, 4)]
    zls = [zl] + [lax.rem(zl + d, 4) for d in range(1, 4)]
    zhs = [zh] + [lax.rem(zh + d, 4) for d in range(1, 4)]
    vs = [v] + [lax.rem(v + d, 16) for d in range(1, 16)]
    at_x = [(g, zl * 4 + to) for to in xs]
    at_y = [(zh * 8 + to * 2 + c, v) for to in ys]
    at_zl = [(g, to * 4 + x) for to in zls]
    at_zh = [(to * 8 + q, v) for to in zhs]
    at_v = [(g, to) for to in vs]
    at_q = [(zh * 8 + lax.rem(q + d, 8), v) for d in range(8)]
    sibling = (zh * 8 + y * 2 + (1 - c), v)

    loads = {}
    for k, (name, src, dst) in enumerate((
        ("act", act_hbm, act), ("down", down_hbm, down), ("hid", hid_hbm, hid), ("resid", resid_hbm, resid),
        ("gain", gain_hbm, gain), ("thead", thead_hbm, thead), ("ids", ids_hbm, ids), ("counts", counts_hbm, counts),
        ("shead", shead_hbm, shead),
    )):
        loads[name] = pltpu.make_async_copy(src, dst, load_sem.at[k])
    for name in ("act", "down", "hid"):
        loads[name].start()

    barrier = pltpu.get_barrier_semaphore()
    for d in range(1, 16):
        pl.semaphore_signal(barrier, inc=1, device_id=at_v[d], device_id_type=MESH)
    for d in range(1, 8):
        pl.semaphore_signal(barrier, inc=1, device_id=at_q[d], device_id_type=MESH)
    for d in range(1, 4):
        pl.semaphore_signal(barrier, inc=1, device_id=at_zh[d], device_id_type=MESH)

    for name in ("resid", "gain", "thead", "ids", "counts", "shead"):
        loads[name].start()

    links = Links(send_sem, recv_sem)

    loads["hid"].wait()
    mine = sl.at[zl, zh]
    mine[...] = jnp.zeros((16, 128), BF16)
    mine[0:12, :] = hid[...]

    pl.semaphore_wait(barrier, 25)
    s_zh = [links.start(mine, mine, at_zh[d]) for d in range(1, 4)]

    loads["act"].wait()
    loads["down"].wait()
    part = lax.dot_general(act[...], down[...], NT, preferred_element_type=F32)
    pmain[...] = part[:, 0:128]
    prem[:, 0:32] = part[:, 128:160]
    lane48 = iota((48, 128), 1) // 32
    packed = jnp.zeros((48, 128), F32)
    for k in range(4):
        rows = prem[pl.ds(k, 48, stride=4), :]
        rows = rows if k == 0 else pltpu.roll(rows, 32 * k, 1)
        packed = jnp.where(lane48 == k, rows, packed)
    ppack[...] = packed
    for vv in range(16):
        psend[vv, 0:12, :] = pmain[12 * vv : 12 * vv + 12, :]
        psend[vv, 12:15, :] = ppack[3 * vv : 3 * vv + 3, :]
        psend[vv, 15:16, :] = jnp.zeros((1, 128), F32)
    sums = [links.start(psend.at[vs[d]], precv.at[d - 1], at_v[d]) for d in range(1, 16)]

    loads["resid"].wait()
    loads["gain"].wait()
    group = iota((16, 128), 1) // 32
    rs[...] = jnp.zeros((16, 256), F32)
    rs[0:12, 0:160] = resid[...].astype(F32)
    gs[...] = jnp.zeros((1, 256), F32)
    gs[:, 0:160] = gain[...]
    four = gs[:, 128:256]
    four = four + pltpu.roll(four, 32, 1)
    four = four + pltpu.roll(four, 64, 1)
    gains = jnp.where(iota((16, 128), 0) < 12, gs[:, 0:128], four)
    rp[...] = rs[:, 0:128]
    for j in range(3):
        line = rs[4 * j : 4 * j + 1, 128:256]
        for k in range(1, 4):
            line = line + pltpu.roll(rs[4 * j + k : 4 * j + k + 1, 128:256], 32 * k, 1)
        rp[12 + j : 13 + j, :] = line
    rem[...] = jnp.zeros((16, 128), F32)
    zs_ref[...] = jnp.zeros((192, TOK), F32)
    zt_ref[...] = jnp.zeros((192, TOK), F32)
    fsend[...] = jnp.zeros((4, 4, 16, 128), BF16)
    fown[...] = jnp.zeros((4, 4, 16, 128), F32)

    arrived(s_zh)
    run = sl.at[zl]
    s_zl = [links.start(run, run, at_zl[d]) for d in range(1, 4)]

    loads["thead"].wait()
    lane = iota((16, 128), 1)

    def reorder(third):
        def rows16(step, carry):
            rows = pl.ds(pl.multiple_of(third * 64 + step * 16, 16), 16)
            for qq in range(8):
                last = jnp.zeros((16, 128), F32)
                off = 32 * (qq % 4)
                for h in range(4):
                    first = ((h * 8 + qq) * 160) // 128
                    right = thead[rows, (first + 1) * 128 : (first + 2) * 128].astype(F32)
                    if off == 0:
                        hp[qq, h, rows, :] = thead[rows, first * 128 : (first + 1) * 128]
                    else:
                        left = thead[rows, first * 128 : (first + 1) * 128].astype(F32)
                        joined = jnp.where(lane < off, right, left)
                        hp[qq, h, rows, :] = pltpu.roll(joined, 128 - off, 1).astype(BF16)
                    shift = (32 * h - off) % 128
                    moved = right if shift == 0 else pltpu.roll(right, shift, 1)
                    last = jnp.where(lane // 32 == h, moved, last)
                hp[qq, 4, rows, :] = last.astype(BF16)
            return carry

        lax.fori_loop(0, 4, rows16, 0)

    reorder(0)

    def pack(src, dst, tiles):
        for j in range(tiles):
            for k in range(4):
                rows48[j, 12 * k : 12 * k + 12, :] = src[k, j].astype(F32)[0:12, :]
        for j in range(tiles):
            dst[c, y, x, 3 * j : 3 * j + 3] = rows48[j].astype(BF16).reshape(3, 16, 128)

    def cut(tiles):
        half = (3 * tiles + 1) // 2
        return pl.ds(0, half), pl.ds(half, 3 * tiles - half)

    def spread(buf, tiles):
        lo, hi = cut(tiles)
        one, two = buf.at[c, y, x, lo], buf.at[c, y, x, hi]
        a = [links.start(one, one, at_x[d]) for d in range(1, 4)]
        b = [links.start(two, two, at_y[d]) for d in range(1, 4)]
        return a, b

    def spread_on(buf, tiles, a, b):
        lo, hi = cut(tiles)
        one, two = buf.at[c, y, :, lo], buf.at[c, :, x, hi]
        arrived(a)
        a = [links.start(one, one, at_y[d]) for d in range(1, 4)]
        arrived(b)
        b = [links.start(two, two, at_x[d]) for d in range(1, 4)]
        return a, b, [links.start(one, one, sibling), links.start(two, two, sibling)]

    def hand_over(buf, tiles, a, b, core):
        lo, hi = cut(tiles)
        for d in (1, 3, 2):
            a[d - 1].wait_recv()
            one = buf.at[c, ys[4 - d], :, lo]
            core.append(links.start(one, one, sibling))
            b[d - 1].wait_recv()
            two = buf.at[c, :, xs[4 - d], hi]
            core.append(links.start(two, two, sibling))

    arrived(sums)
    total = psend[v]
    for d in range(15):
        total = total + precv[d]
    pre = total + rp[...]
    square = pre * pre
    row_of, lane_of = iota((16, 128), 0), iota((16, 128), 1)
    diagonal = row_of == lane_of
    line = jnp.where(diagonal & (row_of < 12), jnp.sum(square, axis=1, keepdims=True), 0.0)
    for k in range(4):
        column = jnp.sum(jnp.where(group == k, square, 0.0), axis=1, keepdims=True)
        line = line + jnp.where((row_of >= 12) & (lane_of == 4 * row_of - 48 + k), column, 0.0)
    u1[q] = jnp.sum(line, axis=0, keepdims=True)
    squares = [links.start(u1.at[q], u1.at[q], at_q[d]) for d in range(1, 8)]

    tz[zh] = pre * gains
    t_zh = [links.start(tz.at[zh], tz.at[zh], at_zh[d]) for d in range(1, 4)]

    arrived(s_zl)
    pack(sl, sg, 4)
    s_a, s_b = spread(sg, 4)

    arrived(squares)
    line = u1[0]
    for k in range(1, 8):
        line = line + u1[k]
    u2[zh] = line
    squares = [links.start(u2.at[zh], u2.at[zh], at_zh[d]) for d in range(1, 4)]
    reorder(1)

    arrived(t_zh)
    for k in range(4):
        side = jnp.zeros((8, 128), F32)
        for h in range(4):
            tail = tz[h, 8:16, :]
            tail = tail if h == k else pltpu.roll(tail, 32 * ((h - k) % 4), 1)
            side = jnp.where(iota((8, 128), 1) // 32 == h, tail, side)
        for j in range(3):
            rem[4 * j + k : 4 * j + k + 1, :] = side[4 + j : 5 + j, :]

    arrived(squares)
    line = (u2[0] + u2[1]) + (u2[2] + u2[3])
    column = jnp.sum(jnp.where(diagonal, line, 0.0), axis=1, keepdims=True)
    scale = lax.rsqrt(column / DT + 1e-06)
    for h in range(4):
        tl[zl, h] = (tz[h] * scale).astype(BF16)
    tl[zl, 4] = (rem[...] * scale).astype(BF16)
    run = tl.at[zl]
    t_zl = [links.start(run, run, at_zl[d]) for d in range(1, 4)]
    s_a, s_b, s_core = spread_on(sg, 4, s_a, s_b)

    arrived(t_zl)
    pack(tl, tg, 5)
    t_a, t_b = spread(tg, 5)
    reorder(2)

    loads["ids"].wait()
    loads["counts"].wait()
    line = iota((1, TOK), 1)
    at = sum((line >= 48 * k).astype(jnp.int32) for k in range(1, 4))
    line = line - 48 * at
    run = sum((line >= 12 * k).astype(jnp.int32) for k in range(1, 4))
    token = run * 48 + at * 12 + line - 12 * run
    chosen = jnp.where(iota((TOK, TOK), 0) == token, 1.0, 0.0).astype(BF16)
    domain = jnp.dot(
        jnp.broadcast_to(ids[...], (8, TOK)).astype(F32).astype(BF16), chosen, preferred_element_type=F32)[0:1]
    counted = jnp.zeros((1, TOK), F32)
    for k in range(NDOM):
        counted = jnp.where(domain == float(k), counts[:, k : k + 1].astype(F32), counted)
    weight = TOK / NDOM / counted

    def rows_of(buf, cc, yy, j):
        return buf[cc, yy, :, 3 * j : 3 * j + 3].reshape(TOK, 128)

    def columns(cc, yy):
        return jnp.concatenate(
            [shead[:, pl.ds(pl.multiple_of((h * 8 + yy * 2 + cc) * 128, 128), 128)] for h in range(4)], axis=1)

    def student(cc):
        def one(yy, carry):
            right = jnp.concatenate([rows_of(sg, cc, yy, h) for h in range(4)], axis=1)
            zs_ref[...] += lax.dot_general(columns(cc, yy), right, NT, preferred_element_type=F32)
            return carry

        lax.fori_loop(0, 4, one, 0)

    def teacher(cc):
        def two(half, carry):
            pairs = [(half * 2 + k, j) for k in range(2) for j in range(5)]
            left = jnp.concatenate([hp[yy * 2 + cc, j] for yy, j in pairs], axis=1)
            right = jnp.concatenate([rows_of(tg, cc, yy, j) for yy, j in pairs], axis=1)
            zt_ref[...] += lax.dot_general(left, right, NT, preferred_element_type=F32)
            return carry

        lax.fori_loop(0, 2, two, 0)

    t_a, t_b, t_core = spread_on(tg, 5, t_a, t_b)
    hand_over(sg, 4, s_a, s_b, s_core)
    loads["shead"].wait()
    student(c)
    arrived(s_core)
    student(1 - c)
    zs = zs_ref[...]
    ms = jnp.max(zs, axis=0, keepdims=True)
    ss = jnp.sum(jnp.exp(zs - ms), axis=0, keepdims=True)
    hand_over(tg, 5, t_a, t_b, t_core)
    teacher(c)
    arrived(t_core)
    teacher(1 - c)
    zs, zt = zs_ref[...], zt_ref[...]
    mt = jnp.max(zt, axis=0, keepdims=True)
    et = jnp.exp(zt - mt)
    stats = (mt, jnp.sum(et, axis=0, keepdims=True), jnp.sum(et * (zt - zs), axis=0, keepdims=True), ms, ss)
    for buf, slot, count, peer in ((q1, v, 16, at_v), (q2, q, 8, at_q), (q3, zh, 4, at_zh)):
        own = buf.at[slot]
        for k in range(5):
            own[k] = stats[k]
        arrived([links.start(own, own, peer[d]) for d in range(1, count)])
        stats = merge(buf, count)
    mt, st, at, ms, ss = stats

    zs, zt = zs_ref[...], zt_ref[...]
    dl = jnp.exp(zs - ms) * (weight / ss) - jnp.exp(zt - mt) * (weight / st)
    dl_ref[...] = jnp.transpose(dl).astype(BF16)

    def blocks(cc, yy):
        return jnp.dot(dl_ref[...], columns(cc, yy), preferred_element_type=F32)

    def row(k):
        return lax.rem(y + k + 1, 4)

    def to_other(k):
        return gsend.at[row(k)], grecv.at[row(k)], sibling

    def along_y(k):
        return gx.at[row(k), :, pl.ds(6, 6)], ryb.at[k], (zh * 8 + row(k) * 2 + c, v)

    o_first, over = links.group(4, to_other)
    b_first, r_b = links.group(3, along_y)

    def give(k, carry):
        piece = blocks(1 - c, row(k))
        for h in range(4):
            gsend[row(k), :, 3 * h : 3 * h + 3] = piece[:, h * 128 : h * 128 + 128].astype(BF16).reshape(4, 3, 16, 128)
        links.at(o_first + k, *to_other(k)).start()
        return carry

    def keep(k, carry):
        piece = blocks(c, row(k))
        links.at(o_first + k, *to_other(k)).wait_recv()
        for h in range(4):
            part = pl.ds(3 * h, 3)
            both = piece[:, h * 128 : h * 128 + 128].reshape(4, 3, 16, 128) + grecv[row(k), :, part].astype(F32)
            gown[row(k), :, part] = both
            gx[row(k), :, part] = both.astype(BF16)

        @pl.when(k < 3)
        def _():
            links.at(b_first + k, *along_y(k)).start()

        return carry

    lax.fori_loop(0, 4, give, 0)
    lax.fori_loop(0, 4, keep, 0)
    r_a = [links.start(gx.at[:, xs[d], pl.ds(0, 6)], rxa.at[d - 1], at_x[d]) for d in range(1, 4)]

    arrived(r_b)
    acc = gown[y, :, 6:12]
    for d in range(3):
        acc = acc + ryb[d].astype(F32)
    gown[y, :, 6:12] = acc
    sb[...] = acc.astype(BF16)
    r_b = [links.start(sb.at[xs[d]], rxb.at[d - 1], at_x[d]) for d in range(1, 4)]
    arrived(r_a)
    acc = gown[:, x, 0:6]
    for d in range(3):
        acc = acc + rxa[d].astype(F32)
    gown[:, x, 0:6] = acc
    sa[...] = acc.astype(BF16)
    r_a = [links.start(sa.at[ys[d]], rya.at[d - 1], at_y[d]) for d in range(1, 4)]

    kl = at / st - mt - jnp.log(st) + ms + jnp.log(ss)
    loss = jnp.zeros((1, NDOM), F32)
    for k in range(NDOM):
        one = jnp.sum(jnp.where(domain == float(k), weight * kl, 0.0), axis=1, keepdims=True)
        loss = jnp.where(iota((1, NDOM), 1) == k, one, loss)
    loss_out[...] = loss

    arrived(r_b)
    acc = gown[y, x, 6:12]
    for d in range(3):
        acc = acc + rxb[d].astype(F32)
    fin[2:4] = acc.reshape(2, 48, 128)
    arrived(r_a)
    acc = gown[y, x, 0:6]
    for d in range(3):
        acc = acc + rya[d].astype(F32)
    fin[0:2] = acc.reshape(2, 48, 128)

    for h in range(4):
        for k in range(4):
            rows = fin[h, 12 * k : 12 * k + 12, :]
            fown[k, h, 0:12, :] = rows
            fsend[k, h, 0:12, :] = rows.astype(BF16)
    last = [links.start(fsend.at[zls[d]], rzl.at[d - 1], at_zl[d]) for d in range(1, 4)]
    links.finish()
    arrived(last)
    acc = fown[zl]
    for d in range(3):
        acc = acc + rzl[d].astype(F32)
    fown[0] = acc
    zsend[...] = acc.astype(BF16)
    arrived([links.start(zsend.at[zhs[d]], rzh.at[d - 1], at_zh[d]) for d in range(1, 4)])
    acc = fown[0, zh]
    for d in range(3):
        acc = acc + rzh[d].astype(F32)
    grad_out[...] = acc[0:12, :]
    links.finish()


def per_device(t_act, t_down, t_resid, t_gain, s_hidden, t_head, s_head, domain_ids, domain_counts):
    anywhere = pl.BlockSpec(memory_space=pltpu.HBM)
    held = pl.BlockSpec(memory_space=pltpu.VMEM)

    def vmem(shape, dtype=F32):
        return pltpu.VMEM(shape, dtype)

    grad, loss = pl.pallas_call(
        body,
        out_shape=(jax.ShapeDtypeStruct((12, 128), F32), jax.ShapeDtypeStruct((1, NDOM), F32)),
        in_specs=[anywhere] * 9,
        out_specs=(held, held),
        scratch_shapes=[
            vmem((192, 1600), BF16), vmem((160, 1600), BF16), vmem((12, 160), BF16), vmem((1, 160)),
            vmem((12, 128), BF16), vmem((192, DT), BF16), vmem((192, DS), BF16), vmem((1, TOK), jnp.int32), vmem((1, NDOM), jnp.int32),
            vmem((192, 128)), vmem((192, 128)), vmem((48, 128)),
            vmem((16, 16, 128)), vmem((15, 16, 128)), vmem((16, 128)),
            vmem((16, 256)), vmem((16, 128)), vmem((1, 256)), vmem((8, 1, 128)), vmem((4, 1, 128)),
            vmem((8, 5, 192, 128), BF16), vmem((4, 16, 128)), vmem((4, 5, 16, 128), BF16),
            vmem((2, 4, 4, 15, 16, 128), BF16), vmem((4, 4, 16, 128), BF16), vmem((2, 4, 4, 12, 16, 128), BF16),
            vmem((5, 48, 128)), vmem((16, 5, 1, TOK)), vmem((8, 5, 1, TOK)), vmem((4, 5, 1, TOK)),
            vmem((192, TOK)), vmem((192, TOK)), vmem((TOK, 192), BF16),
            vmem((4, 4, 12, 16, 128), BF16), vmem((4, 4, 12, 16, 128), BF16),
            vmem((4, 4, 12, 16, 128)), vmem((4, 4, 12, 16, 128), BF16),
            vmem((3, 4, 6, 16, 128), BF16), vmem((3, 4, 6, 16, 128), BF16),
            vmem((3, 6, 16, 128), BF16), vmem((3, 6, 16, 128), BF16),
            vmem((4, 6, 16, 128), BF16), vmem((4, 6, 16, 128), BF16),
            vmem((4, 48, 128)), vmem((4, 4, 16, 128)), vmem((4, 4, 16, 128), BF16), vmem((3, 4, 16, 128), BF16),
            vmem((4, 16, 128), BF16), vmem((3, 16, 128), BF16),
            pltpu.SemaphoreType.DMA((9,)), pltpu.SemaphoreType.DMA((NSEM,)), pltpu.SemaphoreType.DMA((NSEM,)),
        ],
        compiler_params=pltpu.CompilerParams(
            collective_id=0, has_side_effects=True, vmem_limit_bytes=62 * 1024 * 1024),
    )(
        t_act, t_down.T, t_resid, t_gain.reshape(1, -1), s_hidden, t_head, s_head, domain_ids.reshape(1, -1),
        domain_counts.reshape(1, -1),
    )
    return grad, loss.reshape(NDOM)


def solution(mesh):
    return jax.shard_map(
        per_device,
        mesh=mesh,
        in_specs=(
            P(None, "vocab"),
            P("vocab", "grp"),
            P("vocab", "grp"),
            P("grp"),
            P("vocab", "grp"),
            P(("grp", "vocab"), None),
            P(("grp", "vocab"), None),
            P(),
            P(),
        ),
        out_specs=(P("vocab", "grp"), P()),
        check_vma=False,
    )
```

```python
import jax
import jax.numpy as jnp
from jax import lax
from jax.experimental import pallas as pl
from jax.experimental.pallas import tpu as pltpu
from jax.sharding import PartitionSpec as P

DT = 5120
DS = 4096
TOK = 192
NDOM = 8
F32 = jnp.float32
BF16 = jnp.bfloat16
MESH = pl.DeviceIdType.MESH
NSEM = 192
NT = (((1,), (1,)), ((), ()))


def iota(shape, axis):
    return lax.broadcasted_iota(jnp.int32, shape, axis)


class Links:
    def __init__(self, send, recv):
        self.send, self.recv, self.used, self.all = send, recv, 0, []

    def at(self, k, src, dst, device):
        return pltpu.make_async_remote_copy(
            src_ref=src, dst_ref=dst, send_sem=self.send.at[k], recv_sem=self.recv.at[k],
            device_id=device, device_id_type=MESH,
        )

    def start(self, src, dst, device):
        copy = self.at(self.used, src, dst, device)
        self.used += 1
        copy.start()
        self.all.append(copy)
        return copy

    def group(self, count, describe):
        first = self.used
        self.used += count
        copies = [self.at(first + k, *describe(k)) for k in range(count)]
        self.all += copies
        return first, copies

    def finish(self):
        for copy in self.all:
            copy.wait_send()
        self.all = []


def arrived(copies):
    for copy in copies:
        copy.wait_recv()


def merge(buf, count):
    mt, ms = buf[0, 0], buf[0, 3]
    for k in range(1, count):
        mt, ms = jnp.maximum(mt, buf[k, 0]), jnp.maximum(ms, buf[k, 3])
    st = at = ss = jnp.zeros((1, TOK), F32)
    for k in range(count):
        ft, fs = jnp.exp(buf[k, 0] - mt), jnp.exp(buf[k, 3] - ms)
        st, at, ss = st + buf[k, 1] * ft, at + buf[k, 2] * ft, ss + buf[k, 4] * fs
    return mt, st, at, ms, ss


def body(
    act_hbm, down_hbm, resid_hbm, gain_hbm, hid_hbm, thead_hbm, shead_hbm, ids_hbm, counts_hbm,
    grad_out, loss_out,
    act, down, resid, gain, hid, thead, shead, ids, counts,
    pmain, prem, ppack, psend, precv, rem, rs, rp, gs, u1, u2,
    hp, tz, tl, tg, sl, sg, rows48, q1, q2, q3, zs_ref, zt_ref, dl_ref,
    gsend, grecv, gown, gx, rxa, ryb, rya, rxb, sa, sb, fin, fown, fsend, rzl, zsend, rzh,
    load_sem, send_sem, recv_sem,
):
    g, v = lax.axis_index("grp"), lax.axis_index("vocab")
    zh, q = lax.div(g, 8), lax.rem(g, 8)
    y, c = lax.div(q, 2), lax.rem(q, 2)
    zl, x = lax.div(v, 4), lax.rem(v, 4)
    xs = [x] + [lax.rem(x + d, 4) for d in range(1, 4)]
    ys = [y] + [lax.rem(y + d, 4) for d in range(1, 4)]
    zls = [zl] + [lax.rem(zl + d, 4) for d in range(1, 4)]
    zhs = [zh] + [lax.rem(zh + d, 4) for d in range(1, 4)]
    vs = [v] + [lax.rem(v + d, 16) for d in range(1, 16)]
    at_x = [(g, zl * 4 + to) for to in xs]
    at_y = [(zh * 8 + to * 2 + c, v) for to in ys]
    at_zl = [(g, to * 4 + x) for to in zls]
    at_zh = [(to * 8 + q, v) for to in zhs]
    at_v = [(g, to) for to in vs]
    at_q = [(zh * 8 + lax.rem(q + d, 8), v) for d in range(8)]
    sibling = (zh * 8 + y * 2 + (1 - c), v)

    loads = {}
    for k, (name, src, dst) in enumerate((
        ("act", act_hbm, act), ("down", down_hbm, down), ("hid", hid_hbm, hid), ("resid", resid_hbm, resid),
        ("gain", gain_hbm, gain), ("thead", thead_hbm, thead), ("ids", ids_hbm, ids), ("counts", counts_hbm, counts),
        ("shead", shead_hbm, shead),
    )):
        loads[name] = pltpu.make_async_copy(src, dst, load_sem.at[k])
    for name in ("act", "down", "hid"):
        loads[name].start()

    barrier = pltpu.get_barrier_semaphore()
    for d in range(1, 16):
        pl.semaphore_signal(barrier, inc=1, device_id=at_v[d], device_id_type=MESH)
    for d in range(1, 8):
        pl.semaphore_signal(barrier, inc=1, device_id=at_q[d], device_id_type=MESH)
    for d in range(1, 4):
        pl.semaphore_signal(barrier, inc=1, device_id=at_zh[d], device_id_type=MESH)

    for name in ("resid", "gain", "thead", "ids", "counts", "shead"):
        loads[name].start()

    links = Links(send_sem, recv_sem)

    loads["hid"].wait()
    mine = sl.at[zl, zh]
    mine[...] = jnp.zeros((16, 128), BF16)
    mine[0:12, :] = hid[...]

    loads["act"].wait()
    loads["down"].wait()
    part = lax.dot_general(act[...], down[...], NT, preferred_element_type=F32)
    pmain[...] = part[:, 0:128]
    prem[:, 0:32] = part[:, 128:160]
    lane48 = iota((48, 128), 1) // 32
    packed = jnp.zeros((48, 128), F32)
    for k in range(4):
        rows = prem[pl.ds(k, 48, stride=4), :]
        rows = rows if k == 0 else pltpu.roll(rows, 32 * k, 1)
        packed = jnp.where(lane48 == k, rows, packed)
    ppack[...] = packed
    for vv in range(16):
        psend[vv, 0:12, :] = pmain[12 * vv : 12 * vv + 12, :]
        psend[vv, 12:15, :] = ppack[3 * vv : 3 * vv + 3, :]
        psend[vv, 15:16, :] = jnp.zeros((1, 128), F32)
    pl.semaphore_wait(barrier, 25)
    s_zh = [links.start(mine, mine, at_zh[d]) for d in range(1, 4)]

    sums = [links.start(psend.at[vs[d]], precv.at[d - 1], at_v[d]) for d in range(1, 16)]

    loads["resid"].wait()
    loads["gain"].wait()
    group = iota((16, 128), 1) // 32
    rs[...] = jnp.zeros((16, 256), F32)
    rs[0:12, 0:160] = resid[...].astype(F32)
    gs[...] = jnp.zeros((1, 256), F32)
    gs[:, 0:160] = gain[...]
    four = gs[:, 128:256]
    four = four + pltpu.roll(four, 32, 1)
    four = four + pltpu.roll(four, 64, 1)
    gains = jnp.where(iota((16, 128), 0) < 12, gs[:, 0:128], four)
    rp[...] = rs[:, 0:128]
    for j in range(3):
        line = rs[4 * j : 4 * j + 1, 128:256]
        for k in range(1, 4):
            line = line + pltpu.roll(rs[4 * j + k : 4 * j + k + 1, 128:256], 32 * k, 1)
        rp[12 + j : 13 + j, :] = line
    rem[...] = jnp.zeros((16, 128), F32)
    zs_ref[...] = jnp.zeros((192, TOK), F32)
    zt_ref[...] = jnp.zeros((192, TOK), F32)
    fsend[...] = jnp.zeros((4, 4, 16, 128), BF16)
    fown[...] = jnp.zeros((4, 4, 16, 128), F32)

    arrived(s_zh)
    run = sl.at[zl]
    s_zl = [links.start(run, run, at_zl[d]) for d in range(1, 4)]

    loads["thead"].wait()
    lane = iota((16, 128), 1)

    def reorder(third):
        def rows16(step, carry):
            rows = pl.ds(pl.multiple_of(third * 64 + step * 16, 16), 16)
            for qq in range(8):
                last = jnp.zeros((16, 128), F32)
                off = 32 * (qq % 4)
                for h in range(4):
                    first = ((h * 8 + qq) * 160) // 128
                    right = thead[rows, (first + 1) * 128 : (first + 2) * 128].astype(F32)
                    if off == 0:
                        hp[qq, h, rows, :] = thead[rows, first * 128 : (first + 1) * 128]
                    else:
                        left = thead[rows, first * 128 : (first + 1) * 128].astype(F32)
                        joined = jnp.where(lane < off, right, left)
                        hp[qq, h, rows, :] = pltpu.roll(joined, 128 - off, 1).astype(BF16)
                    shift = (32 * h - off) % 128
                    moved = right if shift == 0 else pltpu.roll(right, shift, 1)
                    last = jnp.where(lane // 32 == h, moved, last)
                hp[qq, 4, rows, :] = last.astype(BF16)
            return carry

        lax.fori_loop(0, 4, rows16, 0)

    reorder(0)

    def pack(src, dst, tiles):
        for j in range(tiles):
            for k in range(4):
                rows48[j, 12 * k : 12 * k + 12, :] = src[k, j].astype(F32)[0:12, :]
        for j in range(tiles):
            dst[c, y, x, 3 * j : 3 * j + 3] = rows48[j].astype(BF16).reshape(3, 16, 128)

    def cut(tiles):
        half = (3 * tiles + 1) // 2
        return pl.ds(0, half), pl.ds(half, 3 * tiles - half)

    def spread(buf, tiles):
        lo, hi = cut(tiles)
        one, two = buf.at[c, y, x, lo], buf.at[c, y, x, hi]
        a = [links.start(one, one, at_x[d]) for d in range(1, 4)]
        b = [links.start(two, two, at_y[d]) for d in range(1, 4)]
        return a, b

    def spread_on(buf, tiles, a, b):
        lo, hi = cut(tiles)
        one, two = buf.at[c, y, :, lo], buf.at[c, :, x, hi]
        arrived(a)
        a = [links.start(one, one, at_y[d]) for d in range(1, 4)]
        arrived(b)
        b = [links.start(two, two, at_x[d]) for d in range(1, 4)]
        return a, b, [links.start(one, one, sibling), links.start(two, two, sibling)]

    def hand_over(buf, tiles, a, b, core):
        lo, hi = cut(tiles)
        for d in (1, 3, 2):
            a[d - 1].wait_recv()
            one = buf.at[c, ys[4 - d], :, lo]
            core.append(links.start(one, one, sibling))
            b[d - 1].wait_recv()
            two = buf.at[c, :, xs[4 - d], hi]
            core.append(links.start(two, two, sibling))

    arrived(sums)
    total = psend[v]
    for d in range(15):
        total = total + precv[d]
    pre = total + rp[...]
    square = pre * pre
    row_of, lane_of = iota((16, 128), 0), iota((16, 128), 1)
    diagonal = row_of == lane_of
    line = jnp.where(diagonal & (row_of < 12), jnp.sum(square, axis=1, keepdims=True), 0.0)
    for k in range(4):
        column = jnp.sum(jnp.where(group == k, square, 0.0), axis=1, keepdims=True)
        line = line + jnp.where((row_of >= 12) & (lane_of == 4 * row_of - 48 + k), column, 0.0)
    u1[q] = jnp.sum(line, axis=0, keepdims=True)
    squares = [links.start(u1.at[q], u1.at[q], at_q[d]) for d in range(1, 8)]

    tz[zh] = pre * gains
    t_zh = [links.start(tz.at[zh], tz.at[zh], at_zh[d]) for d in range(1, 4)]

    arrived(s_zl)
    pack(sl, sg, 4)
    s_a, s_b = spread(sg, 4)

    arrived(squares)
    line = u1[0]
    for k in range(1, 8):
        line = line + u1[k]
    u2[zh] = line
    squares = [links.start(u2.at[zh], u2.at[zh], at_zh[d]) for d in range(1, 4)]
    reorder(1)

    arrived(t_zh)
    for k in range(4):
        side = jnp.zeros((8, 128), F32)
        for h in range(4):
            tail = tz[h, 8:16, :]
            tail = tail if h == k else pltpu.roll(tail, 32 * ((h - k) % 4), 1)
            side = jnp.where(iota((8, 128), 1) // 32 == h, tail, side)
        for j in range(3):
            rem[4 * j + k : 4 * j + k + 1, :] = side[4 + j : 5 + j, :]

    arrived(squares)
    line = (u2[0] + u2[1]) + (u2[2] + u2[3])
    column = jnp.sum(jnp.where(diagonal, line, 0.0), axis=1, keepdims=True)
    scale = lax.rsqrt(column / DT + 1e-06)
    for h in range(4):
        tl[zl, h] = (tz[h] * scale).astype(BF16)
    tl[zl, 4] = (rem[...] * scale).astype(BF16)
    run = tl.at[zl]
    t_zl = [links.start(run, run, at_zl[d]) for d in range(1, 4)]
    s_a, s_b, s_core = spread_on(sg, 4, s_a, s_b)

    arrived(t_zl)
    pack(tl, tg, 5)
    t_a, t_b = spread(tg, 5)
    reorder(2)

    loads["ids"].wait()
    loads["counts"].wait()
    line = iota((1, TOK), 1)
    at = sum((line >= 48 * k).astype(jnp.int32) for k in range(1, 4))
    line = line - 48 * at
    run = sum((line >= 12 * k).astype(jnp.int32) for k in range(1, 4))
    token = run * 48 + at * 12 + line - 12 * run
    chosen = jnp.where(iota((TOK, TOK), 0) == token, 1.0, 0.0).astype(BF16)
    domain = jnp.dot(
        jnp.broadcast_to(ids[...], (8, TOK)).astype(F32).astype(BF16), chosen, preferred_element_type=F32)[0:1]
    counted = jnp.zeros((1, TOK), F32)
    for k in range(NDOM):
        counted = jnp.where(domain == float(k), counts[:, k : k + 1].astype(F32), counted)
    weight = TOK / NDOM / counted

    def rows_of(buf, cc, yy, j):
        return buf[cc, yy, :, 3 * j : 3 * j + 3].reshape(TOK, 128)

    def columns(cc, yy):
        return jnp.concatenate(
            [shead[:, pl.ds(pl.multiple_of((h * 8 + yy * 2 + cc) * 128, 128), 128)] for h in range(4)], axis=1)

    def student(cc):
        def one(yy, carry):
            right = jnp.concatenate([rows_of(sg, cc, yy, h) for h in range(4)], axis=1)
            zs_ref[...] += lax.dot_general(columns(cc, yy), right, NT, preferred_element_type=F32)
            return carry

        lax.fori_loop(0, 4, one, 0)

    def teacher(cc):
        def two(half, carry):
            pairs = [(half * 2 + k, j) for k in range(2) for j in range(5)]
            left = jnp.concatenate([hp[yy * 2 + cc, j] for yy, j in pairs], axis=1)
            right = jnp.concatenate([rows_of(tg, cc, yy, j) for yy, j in pairs], axis=1)
            zt_ref[...] += lax.dot_general(left, right, NT, preferred_element_type=F32)
            return carry

        lax.fori_loop(0, 2, two, 0)

    t_a, t_b, t_core = spread_on(tg, 5, t_a, t_b)
    hand_over(sg, 4, s_a, s_b, s_core)
    loads["shead"].wait()
    student(c)
    arrived(s_core)
    student(1 - c)
    zs = zs_ref[...]
    ms = jnp.max(zs, axis=0, keepdims=True)
    ss = jnp.sum(jnp.exp(zs - ms), axis=0, keepdims=True)
    hand_over(tg, 5, t_a, t_b, t_core)
    teacher(c)
    arrived(t_core)
    teacher(1 - c)
    zs, zt = zs_ref[...], zt_ref[...]
    mt = jnp.max(zt, axis=0, keepdims=True)
    et = jnp.exp(zt - mt)
    stats = (mt, jnp.sum(et, axis=0, keepdims=True), jnp.sum(et * (zt - zs), axis=0, keepdims=True), ms, ss)
    for buf, slot, count, peer in ((q1, v, 16, at_v), (q2, q, 8, at_q), (q3, zh, 4, at_zh)):
        own = buf.at[slot]
        for k in range(5):
            own[k] = stats[k]
        arrived([links.start(own, own, peer[d]) for d in range(1, count)])
        stats = merge(buf, count)
    mt, st, at, ms, ss = stats

    zs, zt = zs_ref[...], zt_ref[...]
    dl = jnp.exp(zs - ms) * (weight / ss) - jnp.exp(zt - mt) * (weight / st)
    dl_ref[...] = jnp.transpose(dl).astype(BF16)

    def blocks(cc, yy):
        return jnp.dot(dl_ref[...], columns(cc, yy), preferred_element_type=F32)

    def row(k):
        return lax.rem(y + k + 1, 4)

    def to_other(k):
        return gsend.at[row(k)], grecv.at[row(k)], sibling

    def along_y(k):
        return gx.at[row(k), :, pl.ds(6, 6)], ryb.at[k], (zh * 8 + row(k) * 2 + c, v)

    o_first, over = links.group(4, to_other)
    b_first, r_b = links.group(3, along_y)

    def give(k, carry):
        piece = blocks(1 - c, row(k))
        for h in range(4):
            gsend[row(k), :, 3 * h : 3 * h + 3] = piece[:, h * 128 : h * 128 + 128].astype(BF16).reshape(4, 3, 16, 128)
        links.at(o_first + k, *to_other(k)).start()
        return carry

    def keep(k, carry):
        piece = blocks(c, row(k))
        links.at(o_first + k, *to_other(k)).wait_recv()
        for h in range(4):
            part = pl.ds(3 * h, 3)
            both = piece[:, h * 128 : h * 128 + 128].reshape(4, 3, 16, 128) + grecv[row(k), :, part].astype(F32)
            gown[row(k), :, part] = both
            gx[row(k), :, part] = both.astype(BF16)

        @pl.when(k < 3)
        def _():
            links.at(b_first + k, *along_y(k)).start()

        return carry

    lax.fori_loop(0, 4, give, 0)
    lax.fori_loop(0, 4, keep, 0)
    r_a = [links.start(gx.at[:, xs[d], pl.ds(0, 6)], rxa.at[d - 1], at_x[d]) for d in range(1, 4)]

    arrived(r_b)
    acc = gown[y, :, 6:12]
    for d in range(3):
        acc = acc + ryb[d].astype(F32)
    gown[y, :, 6:12] = acc
    sb[...] = acc.astype(BF16)
    r_b = [links.start(sb.at[xs[d]], rxb.at[d - 1], at_x[d]) for d in range(1, 4)]
    arrived(r_a)
    acc = gown[:, x, 0:6]
    for d in range(3):
        acc = acc + rxa[d].astype(F32)
    gown[:, x, 0:6] = acc
    sa[...] = acc.astype(BF16)
    r_a = [links.start(sa.at[ys[d]], rya.at[d - 1], at_y[d]) for d in range(1, 4)]

    kl = at / st - mt - jnp.log(st) + ms + jnp.log(ss)
    loss = jnp.zeros((1, NDOM), F32)
    for k in range(NDOM):
        one = jnp.sum(jnp.where(domain == float(k), weight * kl, 0.0), axis=1, keepdims=True)
        loss = jnp.where(iota((1, NDOM), 1) == k, one, loss)
    loss_out[...] = loss

    arrived(r_b)
    acc = gown[y, x, 6:12]
    for d in range(3):
        acc = acc + rxb[d].astype(F32)
    fin[2:4] = acc.reshape(2, 48, 128)
    arrived(r_a)
    acc = gown[y, x, 0:6]
    for d in range(3):
        acc = acc + rya[d].astype(F32)
    fin[0:2] = acc.reshape(2, 48, 128)

    for h in range(4):
        for k in range(4):
            rows = fin[h, 12 * k : 12 * k + 12, :]
            fown[k, h, 0:12, :] = rows
            fsend[k, h, 0:12, :] = rows.astype(BF16)
    last = [links.start(fsend.at[zls[d]], rzl.at[d - 1], at_zl[d]) for d in range(1, 4)]
    links.finish()
    arrived(last)
    acc = fown[zl]
    for d in range(3):
        acc = acc + rzl[d].astype(F32)
    fown[0] = acc
    zsend[...] = acc.astype(BF16)
    arrived([links.start(zsend.at[zhs[d]], rzh.at[d - 1], at_zh[d]) for d in range(1, 4)])
    acc = fown[0, zh]
    for d in range(3):
        acc = acc + rzh[d].astype(F32)
    grad_out[...] = acc[0:12, :]
    links.finish()


def per_device(t_act, t_down, t_resid, t_gain, s_hidden, t_head, s_head, domain_ids, domain_counts):
    anywhere = pl.BlockSpec(memory_space=pltpu.HBM)
    held = pl.BlockSpec(memory_space=pltpu.VMEM)

    def vmem(shape, dtype=F32):
        return pltpu.VMEM(shape, dtype)

    grad, loss = pl.pallas_call(
        body,
        out_shape=(jax.ShapeDtypeStruct((12, 128), F32), jax.ShapeDtypeStruct((1, NDOM), F32)),
        in_specs=[anywhere] * 9,
        out_specs=(held, held),
        scratch_shapes=[
            vmem((192, 1600), BF16), vmem((160, 1600), BF16), vmem((12, 160), BF16), vmem((1, 160)),
            vmem((12, 128), BF16), vmem((192, DT), BF16), vmem((192, DS), BF16), vmem((1, TOK), jnp.int32), vmem((1, NDOM), jnp.int32),
            vmem((192, 128)), vmem((192, 128)), vmem((48, 128)),
            vmem((16, 16, 128)), vmem((15, 16, 128)), vmem((16, 128)),
            vmem((16, 256)), vmem((16, 128)), vmem((1, 256)), vmem((8, 1, 128)), vmem((4, 1, 128)),
            vmem((8, 5, 192, 128), BF16), vmem((4, 16, 128)), vmem((4, 5, 16, 128), BF16),
            vmem((2, 4, 4, 15, 16, 128), BF16), vmem((4, 4, 16, 128), BF16), vmem((2, 4, 4, 12, 16, 128), BF16),
            vmem((5, 48, 128)), vmem((16, 5, 1, TOK)), vmem((8, 5, 1, TOK)), vmem((4, 5, 1, TOK)),
            vmem((192, TOK)), vmem((192, TOK)), vmem((TOK, 192), BF16),
            vmem((4, 4, 12, 16, 128), BF16), vmem((4, 4, 12, 16, 128), BF16),
            vmem((4, 4, 12, 16, 128)), vmem((4, 4, 12, 16, 128), BF16),
            vmem((3, 4, 6, 16, 128), BF16), vmem((3, 4, 6, 16, 128), BF16),
            vmem((3, 6, 16, 128), BF16), vmem((3, 6, 16, 128), BF16),
            vmem((4, 6, 16, 128), BF16), vmem((4, 6, 16, 128), BF16),
            vmem((4, 48, 128)), vmem((4, 4, 16, 128)), vmem((4, 4, 16, 128), BF16), vmem((3, 4, 16, 128), BF16),
            vmem((4, 16, 128), BF16), vmem((3, 16, 128), BF16),
            pltpu.SemaphoreType.DMA((9,)), pltpu.SemaphoreType.DMA((NSEM,)), pltpu.SemaphoreType.DMA((NSEM,)),
        ],
        compiler_params=pltpu.CompilerParams(
            collective_id=0, has_side_effects=True, vmem_limit_bytes=62 * 1024 * 1024),
    )(
        t_act, t_down.T, t_resid, t_gain.reshape(1, -1), s_hidden, t_head, s_head, domain_ids.reshape(1, -1),
        domain_counts.reshape(1, -1),
    )
    return grad, loss.reshape(NDOM)


def solution(mesh):
    return jax.shard_map(
        per_device,
        mesh=mesh,
        in_specs=(
            P(None, "vocab"),
            P("vocab", "grp"),
            P("vocab", "grp"),
            P("grp"),
            P("vocab", "grp"),
            P(("grp", "vocab"), None),
            P(("grp", "vocab"), None),
            P(),
            P(),
        ),
        out_specs=(P("vocab", "grp"), P()),
        check_vma=False,
    )
```
